512 devices in a mesh: slab: 16 (over x, y), tile: 32 (over z, core).
Axes of the slice: x: 4, y: 4, z: 16, core: 2. Of those that a mesh axis runs over, the one named last changes fastest.
Arguments:
- slab_starts: float32 [16, 4, 8, 256, 512], P('slab', None, None, 'tile'), may hold values from -6 to 6
- substeps: int32 [16, 32], P('slab', 'tile'), may hold values from 2 to 6
- east_velocity: float32 [8, 256, 512], P(None, 'tile'), may hold values from -0.3 to 0.3
- north_velocity: float32 [8, 256, 512], P(None, 'tile'), may hold values from -0.3 to 0.3
- diffusivity: float32 [8, 256, 512], P(None, 'tile'), may hold values from 0.01 to 0.1
Outputs:
- updated: float32 [16, 4, 8, 256, 512], P('slab', None, None, 'tile')
The draws below stay inside these ranges and needn't reach their ends.
All inputs are finite; a program needn't handle non-finite values.
Results may differ from the reference program's by a relative error of at most 0.0003.
Values sent between devices are 32-bit elements; how exact they have to be, the bound alone decides.
No kernel may reach another device: no remote copies, remote signals or barrier semaphores. Data moves between devices by JAX's collectives and lax.ppermute only.
A program may use at most 64 MiB of HBM per device.

```python
import math
import jax
import jax.numpy as jnp
from jax import lax

TR = 4
LEV = 8
NY = 512
MAXSUB = 6
NX = 256
SLABS = 16
N_TILE = 32


def set_ends(array, own_key, least, largest):
    index_at = [jax.random.randint(jax.random.fold_in(own_key, axis), (), 0, length) for axis, length in enumerate(array.shape)]
    longest = array.shape.index(max(array.shape))
    beside = index_at[:longest] + [(index_at[longest] + 1) % array.shape[longest]] + index_at[longest + 1:]
    return array.at[tuple(index_at)].set(least).at[tuple(beside)].set(largest)


def block_scale(own_key, dims, split, smallest, high):
    gain, own = 1.0, jax.random.fold_in(own_key, 6)
    for dim, parts in split:
        steps = jnp.exp(jax.random.uniform(jax.random.fold_in(own, dim), (parts,), jnp.float32, smallest / len(split), high / len(split)))
        gain = gain * jnp.repeat(steps, dims[dim] // parts).reshape([-1 if axis == dim else 1 for axis in range(len(dims))])
    return gain


def noise(rng, dims, spread, bound, pieces=(), held_as=jnp.bfloat16):
    array = spread * jax.random.normal(rng, dims, jnp.float32)
    if pieces:
        array = array * block_scale(rng, dims, pieces, -0.22, 0.18)
    return jnp.clip(array, -bound, bound).astype(held_as)


def setup_inputs(seed: int = 0) -> dict:
    splits = jax.random.split(jax.random.key(seed), 6)
    return {
        "slab_starts": noise(splits[0], (SLABS, TR, LEV, NX, NY), 1.0, 6.0, ((0, 16), (3, 32)), jnp.float32),
        "substeps": set_ends(jax.random.randint(splits[1], (SLABS, N_TILE), 2, 7), jax.random.fold_in(splits[1], 1), 2, 6).astype(jnp.int32),
        "east_velocity": jnp.clip(jax.random.uniform(splits[2], (LEV, NX, NY), jnp.float32, -0.3, 0.3) * block_scale(splits[2], (LEV, NX, NY), ((1, 32),), -0.4, 0.0), -0.3, 0.3),
        "north_velocity": jnp.clip(jax.random.uniform(splits[3], (LEV, NX, NY), jnp.float32, -0.3, 0.3) * block_scale(splits[3], (LEV, NX, NY), ((1, 32),), -0.4, 0.0), -0.3, 0.3),
        "diffusivity": jnp.clip(jnp.exp(math.log(0.1) - 2.3025851 * jax.random.uniform(splits[4], (LEV, NX, NY), jnp.float32) ** block_scale(splits[4], (LEV, NX, NY), ((1, 32),), -0.2, 0.2)), 0.01, 0.1),
    }


def minmod(first_slope, second_slope):
    return 0.5 * (jnp.sign(first_slope) + jnp.sign(second_slope)) * jnp.minimum(jnp.abs(first_slope), jnp.abs(second_slope))


def face_flux(behind, upwind, downwind, beyond, velocity, fraction):
    limiter = 0.5 * (1.0 - jnp.abs(velocity) * fraction)
    west_value = upwind + limiter * minmod(downwind - upwind, upwind - behind)
    east_value = downwind - limiter * minmod(beyond - downwind, downwind - upwind)
    return jnp.maximum(velocity, 0.0) * west_value + jnp.minimum(velocity, 0.0) * east_value


def fine_step(window, east_faces, north_faces, diffusivity, fraction):
    cells_x = diffusivity.shape[1]
    cells_y = diffusivity.shape[2]
    inner = window[:, :, :, 2:cells_y + 2]
    flux_across = face_flux(inner[:, :, 0:cells_x + 1], inner[:, :, 1:cells_x + 2], inner[:, :, 2:cells_x + 3], inner[:, :, 3:cells_x + 4], east_faces, fraction)
    inner = window[:, :, 2:cells_x + 2, :]
    flux_along = face_flux(inner[..., 0:cells_y + 1], inner[..., 1:cells_y + 2], inner[..., 2:cells_y + 3], inner[..., 3:cells_y + 4], north_faces, fraction)
    center = window[:, :, 2:cells_x + 2, 2:cells_y + 2]
    laplace = (window[:, :, 1:cells_x + 1, 2:cells_y + 2] + window[:, :, 3:cells_x + 3, 2:cells_y + 2]
               + window[:, :, 2:cells_x + 2, 1:cells_y + 1] + window[:, :, 2:cells_x + 2, 3:cells_y + 3] - 4.0 * center)
    rate = -(flux_across[:, :, 1:] - flux_across[:, :, :-1]) - (flux_along[..., 1:] - flux_along[..., :-1]) + diffusivity * laplace
    return center + fraction * rate


def coarse_step(padded, east_faces, north_faces, diffusivity):
    cells_x = diffusivity.shape[1]
    cells_y = diffusivity.shape[2]
    flux_across = (jnp.maximum(east_faces, 0.0) * padded[:, :, 0:cells_x + 1, 1:cells_y + 1]
                   + jnp.minimum(east_faces, 0.0) * padded[:, :, 1:cells_x + 2, 1:cells_y + 1])
    flux_along = (jnp.maximum(north_faces, 0.0) * padded[:, :, 1:cells_x + 1, 0:cells_y + 1]
                  + jnp.minimum(north_faces, 0.0) * padded[:, :, 1:cells_x + 1, 1:cells_y + 2])
    center = padded[:, :, 1:cells_x + 1, 1:cells_y + 1]
    laplace = (padded[:, :, 0:cells_x, 1:cells_y + 1] + padded[:, :, 2:cells_x + 2, 1:cells_y + 1]
               + padded[:, :, 1:cells_x + 1, 0:cells_y] + padded[:, :, 1:cells_x + 1, 2:cells_y + 2] - 4.0 * center)
    return center - (flux_across[:, :, 1:] - flux_across[:, :, :-1]) - (flux_along[..., 1:] - flux_along[..., :-1]) + diffusivity * laplace


def reference(slab_starts, substeps, east_velocity, north_velocity, diffusivity):
    levels, total_x, total_y = diffusivity.shape
    tiles = substeps.shape[1]
    cells_x = total_x // tiles
    east_faces = jnp.concatenate([jnp.zeros((levels, 1, total_y), east_velocity.dtype), east_velocity], axis=1)
    north_faces = jnp.concatenate([jnp.zeros((levels, total_x, 1), north_velocity.dtype), north_velocity], axis=2)
    window_cols = (jnp.arange(tiles, dtype=jnp.int32)[:, None] * cells_x + jnp.arange(cells_x + 4, dtype=jnp.int32)[None, :]).astype(jnp.int32)
    face_cols = (jnp.arange(tiles, dtype=jnp.int32)[:, None] * cells_x + jnp.arange(cells_x + 1, dtype=jnp.int32)[None, :]).astype(jnp.int32)
    east_tiles = jnp.moveaxis(east_faces[:, face_cols], 1, 0)
    north_tiles = jnp.moveaxis(north_faces.reshape(levels, tiles, cells_x, total_y + 1), 1, 0)
    diff_tiles = jnp.moveaxis(diffusivity.reshape(levels, tiles, cells_x, total_y), 1, 0)

    def coarse_global(field):
        padded = jnp.pad(field, ((0, 0), (0, 0), (1, 1), (1, 1)))
        return coarse_step(padded, east_faces, north_faces, diffusivity)

    def slab_difference(inputs):
        start_field, step_counts = inputs
        fraction = 1.0 / step_counts.astype(jnp.float32)
        field = start_field
        for substep in range(MAXSUB):
            padded = jnp.pad(field, ((0, 0), (0, 0), (2, 2), (2, 2)))
            windows = jnp.moveaxis(padded[:, :, window_cols], 2, 0)
            stepped = jax.vmap(fine_step)(windows, east_tiles, north_tiles, diff_tiles, fraction)
            stepped = jnp.moveaxis(stepped, 0, 2).reshape(field.shape)
            active = jnp.repeat(substep < step_counts, cells_x)[None, None, :, None]
            field = jnp.where(active, stepped, field)
        return field - coarse_global(start_field)

    difference = lax.map(slab_difference, (slab_starts, substeps))

    def advance(current, slab_diff):
        advanced = coarse_global(current) + slab_diff
        return advanced, advanced

    _, updated = lax.scan(advance, slab_starts[0], difference)
    return updated
```

```python
import functools

import jax
import jax.numpy as jnp
from jax import lax
from jax.experimental import pallas as pl
from jax.experimental.pallas import tpu as pltpu
from jax.sharding import Mesh, PartitionSpec as P

TR, LEV, X, Y = 4, 8, 8, 512
SUB = 6
SLABS = 16
CHIPS = 16
LANE = 128
PIECES = Y // LANE
REACH = 12
ROWS = 2 * X
EXT = ROWS + 2 * REACH
CHUNK = 40
STATE = 8 * REACH
WIDE = jnp.float32
AXES = ("slab", "z", "core")


def split(value):
    return [value[:, LANE * k : LANE * (k + 1)] for k in range(PIECES)]


def join(parts):
    return jnp.concatenate(parts, axis=1)


def lane(k):
    return slice(LANE * k, LANE * (k + 1))


def from_right(parts):
    turned = [pltpu.roll(part, LANE - 1, 1) for part in parts] + [0.0]
    ends = lax.broadcasted_iota(jnp.int32, (8, LANE), 1) == LANE - 1
    return [jnp.where(ends, turned[k + 1], turned[k]) for k in range(PIECES)]


def from_left(parts):
    turned = [pltpu.roll(part, 1, 1) for part in parts] + [0.0]
    ends = lax.broadcasted_iota(jnp.int32, (8, LANE), 1) == 0
    return [jnp.where(ends, turned[k - 1], turned[k]) for k in range(PIECES)]


def minmod(a, b):
    return jnp.maximum(jnp.minimum(a, b), jnp.minimum(jnp.maximum(a, b), 0.0))


def each(function, *lists):
    return [function(*items) for items in zip(*lists)]


def minus(a, b):
    return each(lambda p, q: p - q, a, b)


def call(kernel, shapes, in_specs, scratch=(), flops=1000000, nbytes=1000000, vmem=24 << 20):
    whole = pl.BlockSpec(memory_space=pltpu.VMEM)
    spaces = {
        "v": whole,
        "s": pl.BlockSpec(memory_space=pltpu.SMEM),
        "h": pl.BlockSpec(memory_space=pl.ANY),
    }
    return pl.pallas_call(
        kernel,
        out_shape=[jax.ShapeDtypeStruct(shape, WIDE) for shape in shapes],
        in_specs=[spaces[kind] for kind in in_specs],
        out_specs=[whole] * len(shapes),
        scratch_shapes=list(scratch),
        compiler_params=pltpu.CompilerParams(vmem_limit_bytes=vmem),
        cost_estimate=pl.CostEstimate(flops=flops, bytes_accessed=nbytes, transcendentals=0),
    )


def to_tiles(array):
    rows = array.shape[0] // 8
    return array.reshape(rows, 8, PIECES, LANE).transpose(0, 2, 1, 3)


def from_tiles(array):
    rows = array.shape[0] // (8 * PIECES)
    return array.reshape(rows, PIECES, 8, LANE).transpose(0, 2, 1, 3).reshape(-1, Y)


def prepare_kernel(count, s_ref, e_ref, n_ref, k_ref, out, held, sems):
    slab = lax.axis_index("slab")
    copies = [pltpu.make_async_copy(s_ref, out.at[:, pl.ds(0, 32), :], sems.at[0])]
    for q, ref in enumerate((e_ref, n_ref, k_ref)):
        copies.append(
            pltpu.make_async_copy(ref, held.at[:, pl.ds(32 * q, 32), :], sems.at[q + 1])
        )
    for copy in copies:
        copy.start()
    for copy in copies[1:]:
        copy.wait()
    number = jnp.full((8, LANE), count[0, 0].astype(WIDE), WIDE)
    row = lax.broadcasted_iota(jnp.int32, (8, LANE), 0)
    held[:, 96:104, :] = jnp.zeros((LEV, 8, LANE), WIDE)
    for level in range(LEV):
        part = held[level, pl.ds(6 * slab, 8), :]
        part = jnp.where(row < 6, part, number)
        for tracer in range(TR):
            out[tracer * LEV + level, 32:40, :] = part
    copies[0].wait()


def state_row(arrived, half, row, k):
    start = (2 * 8 * half + row // 8) * CHUNK + 8 * k + row % 8
    return arrived[pl.ds(start, 8, stride=2 * CHUNK), :]


def arrange_kernel(half, arrived, *refs):
    to_next, to_prev = refs[-2:]
    for i in range(REACH):
        for k in range(PIECES):
            to_next[8 * i : 8 * i + 8, lane(k)] = state_row(arrived, half, i + 4, k)
            to_prev[8 * i : 8 * i + 8, lane(k)] = state_row(arrived, half, i, k)
    if half:
        return
    for n in range(SLABS):
        for core in range(2):
            base = (2 * n + core) * CHUNK + 32
            j = 6 * n
            while j < 6 * n + 6:
                stop = min(6 * n + 6, j // 8 * 8 + 8)
                q, k, x = j // 32, j % 32 // 8, j % 8
                piece = arrived[base + j - 6 * n : base + stop - 6 * n, :]
                at = STATE + 16 * q + 8 * core + x
                to_next[at : at + stop - j, lane(k)] = piece
                to_prev[at : at + stop - j, lane(k)] = piece
                j = stop
    for core in range(2):
        for group in range(2):
            start = (16 * group + core) * CHUNK + 38
            piece = arrived[pl.ds(start, 8, stride=2 * CHUNK), :]
            at = STATE + 48
            to_next[at : at + 8, lane(2 * group + core)] = piece
            to_prev[at : at + 8, lane(2 * group + core)] = piece


def next_offset(n):
    return 8 + sum(15 - m for m in range(n // 8 * 8, n))


def prev_offset(n):
    return sum(15 - m for m in range(n + 1, n // 8 * 8 + 8))


def fine_kernel(half, arrived, mine, low_head, high_head, low, high, *refs):
    out, to_next, to_prev, field, wx, kk, ax, axw, py, my, pq, mq, steps, frac = refs[-14:]

    def edge_state(i, carry):
        at = pl.ds(pl.multiple_of(8 * i, 8), 8)
        field[0, i + 2] = low[at, :]
        field[0, i + 2 + REACH + ROWS] = high[at, :]
        return carry

    lax.fori_loop(0, REACH, edge_state, 0)

    def own_state(r, carry):
        for k in range(PIECES):
            field[0, r + 2 + REACH, :, lane(k)] = state_row(arrived, half, r, k)
        return carry

    lax.fori_loop(0, ROWS, own_state, 0)
    for tile in range(6):
        ref = (low_head, mine, high_head)[tile // 2]
        at = STATE + 48
        number = ref[at : at + 8, lane(2 * half + tile % 2)]
        steps[tile] = number
        frac[tile] = 1.0 / jnp.maximum(number, 1.0)

    def spread_rows(ref, first, shift):
        def one(i, carry):
            for q, target in enumerate((wx, py, kk)):
                row = ref[pl.ds(STATE + 16 * q + first + i, 1), :]
                target[i + first + shift] = jnp.broadcast_to(row, (8, Y))
            return carry

        return one

    lax.fori_loop(0, REACH, spread_rows(low_head, ROWS - REACH, REACH + 2 - ROWS), 0)
    lax.fori_loop(0, ROWS, spread_rows(mine, 0, REACH + 2), 0)
    lax.fori_loop(0, REACH, spread_rows(high_head, 0, REACH + ROWS + 2), 0)

    def limited(size, half_fraction):
        return size * (0.5 - half_fraction * size)

    def coefficients(i, carry):
        r = 4 * i + 2
        part = 0.5 * frac[(r + 2) // 8]
        half_fraction = join([part] * PIECES)
        axw[i] = limited(jnp.abs(wx[r - 1]), half_fraction)
        for j in range(4):
            ax[r + j] = limited(jnp.abs(wx[r + j]), half_fraction)
            north = py[r + j]
            south = join(from_left(split(north)))
            forward, backward = jnp.maximum(north, 0.0), jnp.minimum(south, 0.0)
            py[r + j] = forward
            my[r + j] = backward
            pq[r + j] = limited(forward, half_fraction)
            mq[r + j] = limited(-backward, half_fraction)
        return carry

    lax.fori_loop(0, EXT // 4, coefficients, 0)

    def flux(w, a, here, there, slope_here, slope_there):
        up = w > 0.0
        return w * jnp.where(up, here, there) + a * jnp.where(up, slope_here, slope_there)

    def outgoing(a, b, value, slope):
        return a * value + b * slope

    def block(substep, source, target, index):
        r = 4 * index + 2
        tile = (r + 2) // 8
        f = jnp.where(steps[tile] > substep.astype(WIDE), frac[tile], 0.0)
        c = {i: split(field[source, r + i]) for i in range(-2, 6)}
        dx = {i: minus(c[i + 1], c[i]) for i in range(-2, 5)}
        sx = {i: each(minmod, dx[i], dx[i - 1]) for i in range(-1, 5)}
        fx = {}
        for i in range(-1, 4):
            a = split(ax[r + i] if i >= 0 else axw[index])
            fx[i] = each(flux, split(wx[r + i]), a, c[i], c[i + 1], sx[i], sx[i + 1])
        for i in range(4):
            dy = minus(from_right(c[i]), c[i])
            dy_left = minus(c[i], from_left(c[i]))
            sy = each(minmod, dy, dy_left)
            north = each(outgoing, split(py[r + i]), split(pq[r + i]), c[i], sy)
            south = each(outgoing, split(my[r + i]), split(mq[r + i]), c[i], sy)
            north_left = from_left(north)
            south_right = from_right(south)
            k_row = split(kk[r + i])
            for p in range(PIECES):
                spread = (dx[i][p] - dx[i - 1][p]) + (dy[p] - dy_left[p])
                along = (north_left[p] - north[p]) + (south[p] - south_right[p])
                rate = (fx[i - 1][p] - fx[i][p]) + along + k_row[p] * spread
                field[target, r + i, :, lane(p)] = c[i][p] + f * rate

    def substep_blocks(substep, carry):
        source = jnp.where(substep == 0, 0, 1 + (substep + 1) % 2)
        target = 1 + substep % 2
        first = (substep + 1) // 2
        lax.fori_loop(
            first,
            EXT // 4 - first,
            lambda index, _: block(substep, source, target, index),
            None,
        )
        return carry

    lax.fori_loop(0, SUB, substep_blocks, 0)
    final = 1 + (SUB - 1) % 2
    if half == 0:
        later = jnp.where(lax.broadcasted_iota(jnp.int32, (8, LANE), 0) > 0, 1.0, 0.0)
    else:
        later = jnp.ones((8, LANE), WIDE)

    def upwind(w, here, there):
        return w * jnp.where(w > 0.0, here, there)

    def compare(index, carry):
        r = 2 * index + REACH + 2
        c = {j: split(field[0, r + j]) for j in range(-1, 3)}
        fx = [each(upwind, split(wx[r + j]), c[j], c[j + 1]) for j in (-1, 0, 1)]
        for j in range(2):
            right = from_right(c[j])
            left = from_left(c[j])
            north = each(lambda a, b: a * b, split(py[r + j]), c[j])
            south = each(lambda a, b: a * b, split(my[r + j]), c[j])
            north_left = from_left(north)
            south_right = from_right(south)
            end = split(field[final, r + j])
            k_row = split(kk[r + j])
            i = 2 * index + j
            for p in range(PIECES):
                spread = c[j - 1][p] + c[j + 1][p] + left[p] + right[p] - 4.0 * c[j][p]
                along = (north_left[p] - north[p]) + (south[p] - south_right[p])
                coarse = c[j][p] + (fx[j][p] - fx[j + 1][p]) + along + k_row[p] * spread
                at = (i // 8) * 32 + 8 * p + i % 8
                out[pl.ds(at, 8, stride=64), :] = end[p] - later * coarse
        return carry

    lax.fori_loop(0, ROWS // 2, compare, 0)

    to_next[0:8, :] = jnp.zeros((8, Y), WIDE)
    used = next_offset(8 * half + 7) + 8 - 8 * half
    for ref, filled in ((to_next, used), (to_prev, used - 8)):
        total = ref.shape[0]
        ref[filled:total, :] = jnp.zeros((total - filled, Y), WIDE)
    for n in range(8 * half, min(8 * half + 8, 15)):
        rows = 15 - n
        for k in range(PIECES):

            def piece(first, last, upper):
                at = (2 * (n - 8 * half) + upper) * 32 + 8 * k
                return out[at + first : at + last, :]

            at = next_offset(n)
            if rows > 8:
                to_next[at : at + rows - 8, lane(k)] = piece(16 - rows, 8, 0)
                to_next[at + rows - 8 : at + rows, lane(k)] = piece(0, 8, 1)
            else:
                to_next[at : at + rows, lane(k)] = piece(8 - rows, 8, 1)
            at = prev_offset(n)
            if rows > 8:
                to_prev[at : at + 8, lane(k)] = piece(0, 8, 0)
                to_prev[at + 8 : at + rows, lane(k)] = piece(0, rows - 8, 1)
            else:
                to_prev[at : at + rows, lane(k)] = piece(0, rows, 0)


def from_below(tiles):
    row = lax.broadcasted_iota(jnp.int32, (8, LANE), 0)
    turned = [[pltpu.roll(part, 1, 0) for part in tile] for tile in tiles]
    return [
        [jnp.where(row == 0, turned[max(k - 1, 0)][p], turned[k][p]) for p in range(PIECES)]
        for k in range(len(tiles))
    ]


def from_above(tiles):
    row = lax.broadcasted_iota(jnp.int32, (8, LANE), 0)
    turned = [[pltpu.roll(part, 7, 0) for part in tile] for tile in tiles]
    top = len(tiles) - 1
    return [
        [jnp.where(row == 7, turned[min(k + 1, top)][p], turned[k][p]) for p in range(PIECES)]
        for k in range(len(tiles))
    ]


def rows_at(ref, at):
    return split(ref[at : at + 8, :])


def differences(half, n, own, low, high):
    size = 8 if half else 16
    tiles = []
    if n < 15:
        at = next_offset(n) + 15 - n - size
        tiles += [rows_at(low, at + 8 * k) for k in range(size // 8)]
    at = 16 * (n - 8 * half)
    tiles += [rows_at(own, at), rows_at(own, at + 8)]
    if n < 15:
        at = prev_offset(n)
        tiles += [rows_at(high, at + 8 * k) for k in range(size // 8)]
    return tiles


def advance(value, first, added, stencil, inside, keep=None):
    above, below = from_above(value), from_below(value)
    if keep:
        value, above, below = value[keep], above[keep], below[keep]
        first += keep.start
    result = []
    for k in range(len(value)):
        right, left = from_right(value[k]), from_left(value[k])
        parts = []
        for p in range(PIECES):
            a = [stencil[j, pl.ds(8 * (k + first), 8), lane(p)] for j in range(5)]
            moved = (
                (a[0] * value[k][p] + added[k][p])
                + (a[1] * above[k][p] + a[2] * below[k][p])
                + (a[3] * right[p] + a[4] * left[p])
            )
            parts.append(moved * inside if k + first >= 4 else moved)
        result.append(parts)
    return result


def first_chain_kernel(own, mine, low_head, high_head, low, high, out, stencil, state):
    inside = jnp.where(lax.axis_index("z") < CHIPS - 1, 1.0, 0.0).astype(WIDE)

    def rows_of(q):
        return [
            rows_at(ref, STATE + 16 * q + 8 * upper)
            for ref in (low_head, mine, high_head)
            for upper in range(2)
        ]

    east, north, spread = rows_of(0), rows_of(1), rows_of(2)
    west = from_below(east)
    for k in range(6):
        south = from_left(north[k])
        for p in range(PIECES):
            at = (pl.ds(8 * k, 8), lane(p))
            e, w, n, s, d = east[k][p], west[k][p], north[k][p], south[p], spread[k][p]
            outward = jnp.maximum(e, 0.0) - jnp.minimum(w, 0.0)
            outward = outward + (jnp.maximum(n, 0.0) - jnp.minimum(s, 0.0))
            stencil[0, at[0], at[1]] = 1.0 - outward - 4.0 * d
            stencil[1, at[0], at[1]] = d - jnp.minimum(e, 0.0)
            stencil[2, at[0], at[1]] = d + jnp.maximum(w, 0.0)
            stencil[3, at[0], at[1]] = d - jnp.minimum(n, 0.0)
            stencil[4, at[0], at[1]] = d + jnp.maximum(s, 0.0)

    value = differences(0, 0, own, low, high)
    for n in range(8):
        if n:
            value = advance(value, 0, differences(0, n, own, low, high), stencil, inside)
        for k in range(2):
            out[16 * n + 8 * k : 16 * n + 8 * k + 8, :] = join(value[k + 2])
    for k in range(4):
        state[8 * k : 8 * k + 8, :] = join(value[k + 1])


def second_chain_kernel(own, low, high, done, stencil, state, out):
    inside = jnp.where(lax.axis_index("z") < CHIPS - 1, 1.0, 0.0).astype(WIDE)
    out[0:128, :] = done[...]
    value = [rows_at(state, 8 * k) for k in range(4)]
    for n in range(8, 16):
        added = differences(1, n, own, low, high)
        keep = slice(1, 3) if n == 15 else None
        value = advance(value, 1, added, stencil, inside, keep)
        for k in range(2):
            at = 16 * n + 8 * k
            out[at : at + 8, :] = join(value[k if keep else k + 1])


def device_at(slab, z, core):
    return (slab * CHIPS + z) * 2 + core


def to_chip(array, step):
    route = [
        (device_at(p, z, c), device_at(p, z + step, c))
        for p in range(SLABS)
        for z in range(CHIPS)
        for c in range(2)
        if 0 <= z + step < CHIPS
    ]
    return lax.ppermute(array, AXES, route)


def on_device(slab_starts, substeps, east_velocity, north_velocity, diffusivity):
    fields = to_tiles(slab_starts.reshape(TR * LEV * X, Y)).reshape(TR * LEV, 32, LANE)
    speeds = [
        to_tiles(a.reshape(LEV * X, Y)).reshape(LEV, 32, LANE)
        for a in (east_velocity, north_velocity, diffusivity)
    ]
    (sent,) = call(
        prepare_kernel,
        [(TR * LEV, CHUNK, LANE)],
        "shhhh",
        scratch=[pltpu.VMEM((LEV, 104, LANE), WIDE), pltpu.SemaphoreType.DMA((4,))],
        flops=300000,
        nbytes=2000000,
        vmem=63 << 20,
    )(substeps, fields, *speeds)
    arrived = lax.all_to_all(sent, ("slab", "core"), 0, 0, tiled=True)
    arrived = arrived.reshape(TR * LEV * CHUNK, LANE)

    head = STATE + 56
    next_a, prev_a = call(functools.partial(arrange_kernel, 0), [(head, Y), (head, Y)], "v")(
        arrived
    )
    low_a, high_a = to_chip(next_a, 1), to_chip(prev_a, -1)
    next_b, prev_b = call(
        functools.partial(arrange_kernel, 1), [(STATE, Y), (STATE, Y)], "vh"
    )(arrived, next_a)
    low_b, high_b = to_chip(next_b, 1), to_chip(prev_b, -1)

    rows = pltpu.VMEM((EXT + 4, 8, Y), WIDE)
    scratch = [
        pltpu.VMEM((3, EXT + 4, 8, Y), WIDE),
        rows,
        rows,
        rows,
        pltpu.VMEM((EXT // 4, 8, Y), WIDE),
        rows,
        rows,
        rows,
        rows,
        pltpu.VMEM((6, 8, LANE), WIDE),
        pltpu.VMEM((6, 8, LANE), WIDE),
    ]
    own_a, next_c, prev_c = call(
        functools.partial(fine_kernel, 0),
        [(512, LANE), (104, Y), (104, Y)],
        "vvvvvv",
        scratch=scratch,
        flops=25000000,
        nbytes=3000000,
    )(arrived, next_a, low_a, high_a, low_a, high_a)
    low_c, high_c = to_chip(next_c, 1), to_chip(prev_c, -1)
    own_b, next_d, prev_d = call(
        functools.partial(fine_kernel, 1),
        [(512, LANE), (40, Y), (40, Y)],
        "vvvvvvh",
        scratch=scratch,
        flops=25000000,
        nbytes=3000000,
    )(arrived, next_a, low_a, high_a, low_b, high_b, next_c)
    low_d, high_d = to_chip(next_d, 1), to_chip(prev_d, -1)
    own_a, own_b = [from_tiles(a) for a in (own_a, own_b)]
    done, stencil, state = call(
        first_chain_kernel, [(128, Y), (5, 48, Y), (32, Y)], "vvvvvv", flops=5000000
    )(own_a, next_a, low_a, high_a, low_c, high_c)
    (chain,) = call(second_chain_kernel, [(256, Y)], "vvvvvv", flops=3000000)(
        own_b, low_d, high_d, done, stencil, state
    )
    result = lax.all_to_all(
        chain.reshape(SLABS * 2, 8, Y), ("slab", "core"), 0, 0, tiled=True
    )
    return result.reshape(1, TR, LEV, X, Y)


def solution(mesh):
    fine_mesh = Mesh(mesh.devices.reshape(SLABS, CHIPS, 2), AXES)
    tile = ("z", "core")
    return jax.shard_map(
        on_device,
        mesh=fine_mesh,
        in_specs=(
            P("slab", None, None, tile, None),
            P("slab", tile),
            P(None, tile, None),
            P(None, tile, None),
            P(None, tile, None),
        ),
        out_specs=P("slab", None, None, tile, None),
        check_vma=False,
    )
```

```python
import functools

import jax
import jax.numpy as jnp
from jax import lax
from jax.experimental import pallas as pl
from jax.experimental.pallas import tpu as pltpu
from jax.sharding import Mesh, PartitionSpec as P

TR, LEV, X, Y = 4, 8, 8, 512
SUB = 6
SLABS = 16
CHIPS = 16
LANE = 128
PIECES = Y // LANE
REACH = 12
ROWS = 2 * X
EXT = ROWS + 2 * REACH
CHUNK = 40
STATE = 8 * REACH
WIDE = jnp.float32
AXES = ("slab", "z", "core")


def split(value):
    return [value[:, LANE * k : LANE * (k + 1)] for k in range(PIECES)]


def join(parts):
    return jnp.concatenate(parts, axis=1)


def lane(k):
    return slice(LANE * k, LANE * (k + 1))


def from_right(parts):
    turned = [pltpu.roll(part, LANE - 1, 1) for part in parts] + [0.0]
    ends = lax.broadcasted_iota(jnp.int32, (8, LANE), 1) == LANE - 1
    return [jnp.where(ends, turned[k + 1], turned[k]) for k in range(PIECES)]


def from_left(parts):
    turned = [pltpu.roll(part, 1, 1) for part in parts] + [0.0]
    ends = lax.broadcasted_iota(jnp.int32, (8, LANE), 1) == 0
    return [jnp.where(ends, turned[k - 1], turned[k]) for k in range(PIECES)]


def minmod(a, b):
    return jnp.maximum(jnp.minimum(a, b), jnp.minimum(jnp.maximum(a, b), 0.0))


def each(function, *lists):
    return [function(*items) for items in zip(*lists)]


def minus(a, b):
    return each(lambda p, q: p - q, a, b)


def call(kernel, shapes, in_specs, scratch=(), flops=1000000, nbytes=1000000, vmem=24 << 20):
    whole = pl.BlockSpec(memory_space=pltpu.VMEM)
    spaces = {
        "v": whole,
        "s": pl.BlockSpec(memory_space=pltpu.SMEM),
        "h": pl.BlockSpec(memory_space=pl.ANY),
    }
    return pl.pallas_call(
        kernel,
        out_shape=[jax.ShapeDtypeStruct(shape, WIDE) for shape in shapes],
        in_specs=[spaces[kind] for kind in in_specs],
        out_specs=[whole] * len(shapes),
        scratch_shapes=list(scratch),
        compiler_params=pltpu.CompilerParams(vmem_limit_bytes=vmem),
        cost_estimate=pl.CostEstimate(flops=flops, bytes_accessed=nbytes, transcendentals=0),
    )


def to_tiles(array):
    rows = array.shape[0] // 8
    return array.reshape(rows, 8, PIECES, LANE).transpose(0, 2, 1, 3)


def from_tiles(array):
    rows = array.shape[0] // (8 * PIECES)
    return array.reshape(rows, PIECES, 8, LANE).transpose(0, 2, 1, 3).reshape(-1, Y)


def prepare_kernel(count_ref, s_ref, e_ref, n_ref, k_ref, out, held, count, sems):
    slab = lax.axis_index("slab")
    copies = [pltpu.make_async_copy(s_ref, out.at[:, pl.ds(0, 32), :], sems.at[0])]
    for q, ref in enumerate((e_ref, n_ref, k_ref)):
        copies.append(
            pltpu.make_async_copy(ref, held.at[:, pl.ds(32 * q, 32), :], sems.at[q + 1])
        )
    copies.append(pltpu.make_async_copy(count_ref, count, sems.at[4]))
    for copy in copies:
        copy.start()
    for copy in copies[1:]:
        copy.wait()
    number = jnp.broadcast_to(count[...].astype(WIDE), (8, LANE))
    row = lax.broadcasted_iota(jnp.int32, (8, LANE), 0)
    held[:, 96:104, :] = jnp.zeros((LEV, 8, LANE), WIDE)
    for level in range(LEV):
        part = held[level, pl.ds(6 * slab, 8), :]
        part = jnp.where(row < 6, part, number)
        for tracer in range(TR):
            out[tracer * LEV + level, 32:40, :] = part
    copies[0].wait()


def state_row(arrived, half, row, k):
    start = (2 * 8 * half + row // 8) * CHUNK + 8 * k + row % 8
    return arrived[pl.ds(start, 8, stride=2 * CHUNK), :]


def arrange_kernel(half, arrived, *refs):
    to_next, to_prev = refs[-2:]
    for i in range(REACH):
        for k in range(PIECES):
            to_next[8 * i : 8 * i + 8, lane(k)] = state_row(arrived, half, i + 4, k)
            to_prev[8 * i : 8 * i + 8, lane(k)] = state_row(arrived, half, i, k)
    if half:
        return
    for n in range(SLABS):
        for core in range(2):
            base = (2 * n + core) * CHUNK + 32
            j = 6 * n
            while j < 6 * n + 6:
                stop = min(6 * n + 6, j // 8 * 8 + 8)
                q, k, x = j // 32, j % 32 // 8, j % 8
                piece = arrived[base + j - 6 * n : base + stop - 6 * n, :]
                at = STATE + 16 * q + 8 * core + x
                to_next[at : at + stop - j, lane(k)] = piece
                to_prev[at : at + stop - j, lane(k)] = piece
                j = stop
    for core in range(2):
        for group in range(2):
            start = (16 * group + core) * CHUNK + 38
            piece = arrived[pl.ds(start, 8, stride=2 * CHUNK), :]
            at = STATE + 48
            to_next[at : at + 8, lane(2 * group + core)] = piece
            to_prev[at : at + 8, lane(2 * group + core)] = piece


def next_offset(n):
    return 8 + sum(15 - m for m in range(n // 8 * 8, n))


def prev_offset(n):
    return sum(15 - m for m in range(n + 1, n // 8 * 8 + 8))


def fine_kernel(half, arrived, mine, low_head, high_head, low, high, *refs):
    out, to_next, to_prev, field, other, coarse, wx, kk, ax, axw, py, my, pq, mq, steps, frac = refs[-16:]

    def edge_state(i, carry):
        at = pl.ds(pl.multiple_of(8 * i, 8), 8)
        field[i + 2] = low[at, :]
        field[i + 2 + REACH + ROWS] = high[at, :]
        return carry

    lax.fori_loop(0, REACH, edge_state, 0)

    def own_state(r, carry):
        for k in range(PIECES):
            field[r + 2 + REACH, :, lane(k)] = state_row(arrived, half, r, k)
        return carry

    lax.fori_loop(0, ROWS, own_state, 0)
    for tile in range(6):
        ref = (low_head, mine, high_head)[tile // 2]
        at = STATE + 48
        number = ref[at : at + 8, lane(2 * half + tile % 2)]
        steps[tile] = number
        frac[tile] = 1.0 / jnp.maximum(number, 1.0)

    def spread_rows(ref, first, shift):
        def one(i, carry):
            for q, target in enumerate((wx, py, kk)):
                row = ref[pl.ds(STATE + 16 * q + first + i, 1), :]
                target[i + first + shift] = jnp.broadcast_to(row, (8, Y))
            return carry

        return one

    lax.fori_loop(0, REACH, spread_rows(low_head, ROWS - REACH, REACH + 2 - ROWS), 0)
    lax.fori_loop(0, ROWS, spread_rows(mine, 0, REACH + 2), 0)
    lax.fori_loop(0, REACH, spread_rows(high_head, 0, REACH + ROWS + 2), 0)

    def limited(size, half_fraction):
        return size * (0.5 - half_fraction * size)

    def coefficients(i, carry):
        r = 4 * i + 2
        part = 0.5 * frac[(r + 2) // 8]
        half_fraction = join([part] * PIECES)
        axw[i] = limited(jnp.abs(wx[r - 1]), half_fraction)
        for j in range(4):
            ax[r + j] = limited(jnp.abs(wx[r + j]), half_fraction)
            north = py[r + j]
            south = join(from_left(split(north)))
            forward, backward = jnp.maximum(north, 0.0), jnp.minimum(south, 0.0)
            py[r + j] = forward
            my[r + j] = backward
            pq[r + j] = limited(forward, half_fraction)
            mq[r + j] = limited(-backward, half_fraction)
        return carry

    lax.fori_loop(0, EXT // 4, coefficients, 0)

    def flux(w, a, here, there, slope_here, slope_there):
        up = w > 0.0
        return w * jnp.where(up, here, there) + a * jnp.where(up, slope_here, slope_there)

    def outgoing(a, b, value, slope):
        return a * value + b * slope

    def block(substep, source, target, index):
        r = 4 * index + 2
        active = [
            jnp.where(steps[tile] > substep.astype(WIDE), frac[tile], 0.0)
            for tile in ((r + 2) // 8, (r + 6) // 8)
        ]
        c = {i: split(source[r + i]) for i in (-2, -1, 0, 1)}
        dx = {i: minus(c[i + 1], c[i]) for i in (-2, -1, 0)}
        sx = {i: each(minmod, dx[i], dx[i - 1]) for i in (-1, 0)}
        east = None
        for i in range(8):
            c[i + 2] = split(source[r + i + 2])
            dx[i + 1] = minus(c[i + 2], c[i + 1])
            sx[i + 1] = each(minmod, dx[i + 1], dx[i])
            west = east
            if i % 4 == 0:
                a = split(axw[index + i // 4])
                west = each(flux, split(wx[r + i - 1]), a, c[i - 1], c[i], sx[i - 1], sx[i])
            a = split(ax[r + i])
            east = each(flux, split(wx[r + i]), a, c[i], c[i + 1], sx[i], sx[i + 1])
            dy = minus(from_right(c[i]), c[i])
            dy_left = minus(c[i], from_left(c[i]))
            sy = each(minmod, dy, dy_left)
            north = each(outgoing, split(py[r + i]), split(pq[r + i]), c[i], sy)
            south = each(outgoing, split(my[r + i]), split(mq[r + i]), c[i], sy)
            north_left = from_left(north)
            south_right = from_right(south)
            k_row = split(kk[r + i])
            for p in range(PIECES):
                spread = (dx[i][p] - dx[i - 1][p]) + (dy[p] - dy_left[p])
                along = (north_left[p] - north[p]) + (south[p] - south_right[p])
                rate = (west[p] - east[p]) + along + k_row[p] * spread
                target[r + i, :, lane(p)] = c[i][p] + active[i // 4] * rate

    def upwind(w, here, there):
        return w * jnp.where(w > 0.0, here, there)

    def coarse_rows(index, carry):
        r = 2 * index + REACH + 2
        c = {j: split(field[r + j]) for j in range(-1, 3)}
        fx = [each(upwind, split(wx[r + j]), c[j], c[j + 1]) for j in (-1, 0, 1)]
        for j in range(2):
            right = from_right(c[j])
            left = from_left(c[j])
            north = each(lambda a, b: a * b, split(py[r + j]), c[j])
            south = each(lambda a, b: a * b, split(my[r + j]), c[j])
            north_left = from_left(north)
            south_right = from_right(south)
            k_row = split(kk[r + j])
            for p in range(PIECES):
                spread = c[j - 1][p] + c[j + 1][p] + left[p] + right[p] - 4.0 * c[j][p]
                along = (north_left[p] - north[p]) + (south[p] - south_right[p])
                coarse[2 * index + j, :, lane(p)] = (
                    c[j][p] + (fx[j][p] - fx[j + 1][p]) + along + k_row[p] * spread
                )
        return carry

    lax.fori_loop(0, ROWS // 2, coarse_rows, 0)

    def two_substeps(j, carry):
        for odd, source, target in ((0, field, other), (1, other, field)):
            lax.fori_loop(
                0,
                5 - j - odd,
                lambda i, _: block(2 * j + odd, source, target, j + odd + 2 * i),
                None,
            )
        return carry

    lax.fori_loop(0, SUB // 2, two_substeps, 0)
    if half == 0:
        later = jnp.where(lax.broadcasted_iota(jnp.int32, (8, LANE), 0) > 0, 1.0, 0.0)
    else:
        later = jnp.ones((8, LANE), WIDE)

    def finish(index, carry):
        for j in range(4):
            i = 4 * index + j
            for p in range(PIECES):
                at = (i // 8) * 32 + 8 * p + i % 8
                end = field[REACH + 2 + i, :, lane(p)]
                out[pl.ds(at, 8, stride=64), :] = end - later * coarse[i, :, lane(p)]
        return carry

    lax.fori_loop(0, ROWS // 4, finish, 0)

    to_next[0:8, :] = jnp.zeros((8, Y), WIDE)
    used = next_offset(8 * half + 7) + 8 - 8 * half
    for ref, filled in ((to_next, used), (to_prev, used - 8)):
        total = ref.shape[0]
        ref[filled:total, :] = jnp.zeros((total - filled, Y), WIDE)
    for n in range(8 * half, min(8 * half + 8, 15)):
        rows = 15 - n
        for k in range(PIECES):

            def piece(first, last, upper):
                at = (2 * (n - 8 * half) + upper) * 32 + 8 * k
                return out[at + first : at + last, :]

            at = next_offset(n)
            if rows > 8:
                to_next[at : at + rows - 8, lane(k)] = piece(16 - rows, 8, 0)
                to_next[at + rows - 8 : at + rows, lane(k)] = piece(0, 8, 1)
            else:
                to_next[at : at + rows, lane(k)] = piece(8 - rows, 8, 1)
            at = prev_offset(n)
            if rows > 8:
                to_prev[at : at + 8, lane(k)] = piece(0, 8, 0)
                to_prev[at + 8 : at + rows, lane(k)] = piece(0, rows - 8, 1)
            else:
                to_prev[at : at + rows, lane(k)] = piece(0, rows, 0)


def from_below(tiles):
    row = lax.broadcasted_iota(jnp.int32, (8, LANE), 0)
    turned = [[pltpu.roll(part, 1, 0) for part in tile] for tile in tiles]
    return [
        [jnp.where(row == 0, turned[max(k - 1, 0)][p], turned[k][p]) for p in range(PIECES)]
        for k in range(len(tiles))
    ]


def from_above(tiles):
    row = lax.broadcasted_iota(jnp.int32, (8, LANE), 0)
    turned = [[pltpu.roll(part, 7, 0) for part in tile] for tile in tiles]
    top = len(tiles) - 1
    return [
        [jnp.where(row == 7, turned[min(k + 1, top)][p], turned[k][p]) for p in range(PIECES)]
        for k in range(len(tiles))
    ]


def rows_at(ref, at):
    return split(ref[at : at + 8, :])


def differences(half, n, own, low, high):
    size = 8 if half else 16
    tiles = []
    if n < 15:
        at = next_offset(n) + 15 - n - size
        tiles += [rows_at(low, at + 8 * k) for k in range(size // 8)]
    at = 16 * (n - 8 * half)
    tiles += [rows_at(own, at), rows_at(own, at + 8)]
    if n < 15:
        at = prev_offset(n)
        tiles += [rows_at(high, at + 8 * k) for k in range(size // 8)]
    return tiles


def advance(value, first, added, stencil, inside, keep=None):
    above, below = from_above(value), from_below(value)
    if keep:
        value, above, below = value[keep], above[keep], below[keep]
        first += keep.start
    result = []
    for k in range(len(value)):
        right, left = from_right(value[k]), from_left(value[k])
        parts = []
        for p in range(PIECES):
            a = [stencil[j, pl.ds(8 * (k + first), 8), lane(p)] for j in range(5)]
            moved = (
                (a[0] * value[k][p] + added[k][p])
                + (a[1] * above[k][p] + a[2] * below[k][p])
                + (a[3] * right[p] + a[4] * left[p])
            )
            parts.append(moved * inside if k + first >= 4 else moved)
        result.append(parts)
    return result


def first_chain_kernel(own, mine, low_head, high_head, low, high, out, stencil, state):
    inside = jnp.where(lax.axis_index("z") < CHIPS - 1, 1.0, 0.0).astype(WIDE)

    def rows_of(q):
        return [
            rows_at(ref, STATE + 16 * q + 8 * upper)
            for ref in (low_head, mine, high_head)
            for upper in range(2)
        ]

    east, north, spread = rows_of(0), rows_of(1), rows_of(2)
    west = from_below(east)
    for k in range(6):
        south = from_left(north[k])
        for p in range(PIECES):
            at = (pl.ds(8 * k, 8), lane(p))
            e, w, n, s, d = east[k][p], west[k][p], north[k][p], south[p], spread[k][p]
            outward = jnp.maximum(e, 0.0) - jnp.minimum(w, 0.0)
            outward = outward + (jnp.maximum(n, 0.0) - jnp.minimum(s, 0.0))
            stencil[0, at[0], at[1]] = 1.0 - outward - 4.0 * d
            stencil[1, at[0], at[1]] = d - jnp.minimum(e, 0.0)
            stencil[2, at[0], at[1]] = d + jnp.maximum(w, 0.0)
            stencil[3, at[0], at[1]] = d - jnp.minimum(n, 0.0)
            stencil[4, at[0], at[1]] = d + jnp.maximum(s, 0.0)

    value = differences(0, 0, own, low, high)
    for n in range(8):
        if n:
            value = advance(value, 0, differences(0, n, own, low, high), stencil, inside)
        for k in range(2):
            out[16 * n + 8 * k : 16 * n + 8 * k + 8, :] = join(value[k + 2])
    for k in range(4):
        state[8 * k : 8 * k + 8, :] = join(value[k + 1])


def second_chain_kernel(own, low, high, done, stencil, state, out):
    inside = jnp.where(lax.axis_index("z") < CHIPS - 1, 1.0, 0.0).astype(WIDE)
    out[0:128, :] = done[...]
    value = [rows_at(state, 8 * k) for k in range(4)]
    for n in range(8, 16):
        added = differences(1, n, own, low, high)
        keep = slice(1, 3) if n == 15 else None
        value = advance(value, 1, added, stencil, inside, keep)
        for k in range(2):
            at = 16 * n + 8 * k
            out[at : at + 8, :] = join(value[k if keep else k + 1])


def device_at(slab, z, core):
    return (slab * CHIPS + z) * 2 + core


def to_chip(array, step):
    route = [
        (device_at(p, z, c), device_at(p, z + step, c))
        for p in range(SLABS)
        for z in range(CHIPS)
        for c in range(2)
        if 0 <= z + step < CHIPS
    ]
    return lax.ppermute(array, AXES, route)


def on_device(slab_starts, substeps, east_velocity, north_velocity, diffusivity):
    fields = to_tiles(slab_starts.reshape(TR * LEV * X, Y)).reshape(TR * LEV, 32, LANE)
    speeds = [
        to_tiles(a.reshape(LEV * X, Y)).reshape(LEV, 32, LANE)
        for a in (east_velocity, north_velocity, diffusivity)
    ]
    (sent,) = call(
        prepare_kernel,
        [(TR * LEV, CHUNK, LANE)],
        "hhhhh",
        scratch=[
            pltpu.VMEM((LEV, 104, LANE), WIDE),
            pltpu.VMEM((1, 1), jnp.int32),
            pltpu.SemaphoreType.DMA((5,)),
        ],
        flops=300000,
        nbytes=2000000,
        vmem=63 << 20,
    )(substeps, fields, *speeds)
    arrived = lax.all_to_all(sent, ("slab", "core"), 0, 0, tiled=True)
    arrived = arrived.reshape(TR * LEV * CHUNK, LANE)

    head = STATE + 56
    next_a, prev_a = call(functools.partial(arrange_kernel, 0), [(head, Y), (head, Y)], "v")(
        arrived
    )
    low_a, high_a = to_chip(next_a, 1), to_chip(prev_a, -1)
    next_b, prev_b = call(
        functools.partial(arrange_kernel, 1), [(STATE, Y), (STATE, Y)], "vh"
    )(arrived, next_a)
    low_b, high_b = to_chip(next_b, 1), to_chip(prev_b, -1)

    rows = pltpu.VMEM((EXT + 4, 8, Y), WIDE)
    scratch = [
        rows,
        rows,
        pltpu.VMEM((ROWS, 8, Y), WIDE),
        rows,
        rows,
        rows,
        pltpu.VMEM((EXT // 4, 8, Y), WIDE),
        rows,
        rows,
        rows,
        rows,
        pltpu.VMEM((6, 8, LANE), WIDE),
        pltpu.VMEM((6, 8, LANE), WIDE),
    ]
    own_a, next_c, prev_c = call(
        functools.partial(fine_kernel, 0),
        [(512, LANE), (104, Y), (104, Y)],
        "vvvvvv",
        scratch=scratch,
        flops=25000000,
        nbytes=3000000,
    )(arrived, next_a, low_a, high_a, low_a, high_a)
    low_c, high_c = to_chip(next_c, 1), to_chip(prev_c, -1)
    own_b, next_d, prev_d = call(
        functools.partial(fine_kernel, 1),
        [(512, LANE), (40, Y), (40, Y)],
        "vvvvvvh",
        scratch=scratch,
        flops=25000000,
        nbytes=3000000,
    )(arrived, next_a, low_a, high_a, low_b, high_b, next_c)
    low_d, high_d = to_chip(next_d, 1), to_chip(prev_d, -1)
    own_a, own_b = [from_tiles(a) for a in (own_a, own_b)]
    done, stencil, state = call(
        first_chain_kernel, [(128, Y), (5, 48, Y), (32, Y)], "vvvvvv", flops=5000000
    )(own_a, next_a, low_a, high_a, low_c, high_c)
    (chain,) = call(second_chain_kernel, [(256, Y)], "vvvvvv", flops=3000000)(
        own_b, low_d, high_d, done, stencil, state
    )
    result = lax.all_to_all(
        chain.reshape(SLABS * 2, 8, Y), ("slab", "core"), 0, 0, tiled=True
    )
    return result.reshape(1, TR, LEV, X, Y)


def solution(mesh):
    fine_mesh = Mesh(mesh.devices.reshape(SLABS, CHIPS, 2), AXES)
    tile = ("z", "core")
    return jax.shard_map(
        on_device,
        mesh=fine_mesh,
        in_specs=(
            P("slab", None, None, tile, None),
            P("slab", tile),
            P(None, tile, None),
            P(None, tile, None),
            P(None, tile, None),
        ),
        out_specs=P("slab", None, None, tile, None),
        check_vma=False,
    )
```

```python
import functools

import jax
import jax.numpy as jnp
from jax import lax
from jax.experimental import pallas as pl
from jax.experimental.pallas import tpu as pltpu
from jax.sharding import Mesh, PartitionSpec as P

TR, LEV, X, Y = 4, 8, 8, 512
SUB = 6
SLABS = 16
CHIPS = 16
LANE = 128
PIECES = Y // LANE
REACH = 12
ROWS = 2 * X
EXT = ROWS + 2 * REACH
CHUNK = 40
STATE = 8 * REACH
WIDE_HALO, NARROW_HALO = 104, 40
WIDE = jnp.float32
AXES = ("slab", "z", "core")


def split(value):
    return [value[:, LANE * k : LANE * (k + 1)] for k in range(PIECES)]


def join(parts):
    return jnp.concatenate(parts, axis=1)


def lane(k):
    return slice(LANE * k, LANE * (k + 1))


def from_right(parts):
    turned = [pltpu.roll(part, LANE - 1, 1) for part in parts] + [0.0]
    ends = lax.broadcasted_iota(jnp.int32, (8, LANE), 1) == LANE - 1
    return [jnp.where(ends, turned[k + 1], turned[k]) for k in range(PIECES)]


def from_left(parts):
    turned = [pltpu.roll(part, 1, 1) for part in parts] + [0.0]
    ends = lax.broadcasted_iota(jnp.int32, (8, LANE), 1) == 0
    return [jnp.where(ends, turned[k - 1], turned[k]) for k in range(PIECES)]


def minmod(a, b):
    return jnp.maximum(jnp.minimum(a, b), jnp.minimum(jnp.maximum(a, b), 0.0))


def each(function, *lists):
    return [function(*items) for items in zip(*lists)]


def minus(a, b):
    return each(lambda p, q: p - q, a, b)


def call(kernel, shapes, in_specs, scratch=(), flops=1000000, nbytes=1000000, vmem=24 << 20):
    whole = pl.BlockSpec(memory_space=pltpu.VMEM)
    spaces = {
        "v": whole,
        "s": pl.BlockSpec(memory_space=pltpu.SMEM),
        "h": pl.BlockSpec(memory_space=pl.ANY),
    }
    return pl.pallas_call(
        kernel,
        out_shape=[jax.ShapeDtypeStruct(shape, WIDE) for shape in shapes],
        in_specs=[spaces[kind] for kind in in_specs],
        out_specs=[whole] * len(shapes),
        scratch_shapes=list(scratch),
        compiler_params=pltpu.CompilerParams(vmem_limit_bytes=vmem),
        cost_estimate=pl.CostEstimate(flops=flops, bytes_accessed=nbytes, transcendentals=0),
    )


def to_tiles(array):
    rows = array.shape[0] // 8
    return array.reshape(rows, 8, PIECES, LANE).transpose(0, 2, 1, 3)


def from_tiles(array):
    rows = array.shape[0] // (8 * PIECES)
    return array.reshape(rows, PIECES, 8, LANE).transpose(0, 2, 1, 3).reshape(-1, Y)


def prepare_kernel(count_ref, s_ref, e_ref, n_ref, k_ref, out, held, count, sems):
    slab = lax.axis_index("slab")
    copies = [pltpu.make_async_copy(s_ref, out.at[:, pl.ds(0, 32), :], sems.at[0])]
    for q, ref in enumerate((e_ref, n_ref, k_ref)):
        copies.append(
            pltpu.make_async_copy(ref, held.at[:, pl.ds(32 * q, 32), :], sems.at[q + 1])
        )
    copies.append(pltpu.make_async_copy(count_ref, count, sems.at[4]))
    for copy in copies:
        copy.start()
    for copy in copies[1:]:
        copy.wait()
    number = jnp.broadcast_to(count[...].astype(WIDE), (8, LANE))
    row = lax.broadcasted_iota(jnp.int32, (8, LANE), 0)
    held[:, 96:104, :] = jnp.zeros((LEV, 8, LANE), WIDE)
    for level in range(LEV):
        part = held[level, pl.ds(6 * slab, 8), :]
        part = jnp.where(row < 6, part, number)
        for tracer in range(TR):
            out[tracer * LEV + level, 32:40, :] = part
    copies[0].wait()


def state_row(arrived, half, row, k):
    start = (2 * 8 * half + row // 8) * CHUNK + 8 * k + row % 8
    return arrived[pl.ds(start, 8, stride=2 * CHUNK), :]


def arrange_kernel(half, arrived, *refs):
    to_next, to_prev = refs[-2:]
    for i in range(REACH):
        for k in range(PIECES):
            to_next[8 * i : 8 * i + 8, lane(k)] = state_row(arrived, half, i + 4, k)
            to_prev[8 * i : 8 * i + 8, lane(k)] = state_row(arrived, half, i, k)
    if half:
        return
    for n in range(SLABS):
        for core in range(2):
            base = (2 * n + core) * CHUNK + 32
            j = 6 * n
            while j < 6 * n + 6:
                stop = min(6 * n + 6, j // 8 * 8 + 8)
                q, k, x = j // 32, j % 32 // 8, j % 8
                piece = arrived[base + j - 6 * n : base + stop - 6 * n, :]
                at = STATE + 16 * q + 8 * core + x
                to_next[at : at + stop - j, lane(k)] = piece
                to_prev[at : at + stop - j, lane(k)] = piece
                j = stop
    for core in range(2):
        for group in range(2):
            start = (16 * group + core) * CHUNK + 38
            piece = arrived[pl.ds(start, 8, stride=2 * CHUNK), :]
            at = STATE + 48
            to_next[at : at + 8, lane(2 * group + core)] = piece
            to_prev[at : at + 8, lane(2 * group + core)] = piece


def next_offset(n):
    return 8 + sum(15 - m for m in range(n // 8 * 8, n))


def prev_offset(n):
    return sum(15 - m for m in range(n + 1, n // 8 * 8 + 8))


def fine_kernel(half, arrived, mine, low_head, high_head, low, high, *refs):
    field, other, coarse, wx, kk, ax, axw, py, my, pq, mq, steps, frac = refs[-13:]
    for tile in range(6):
        ref = (low_head, mine, high_head)[tile // 2]
        at = STATE + 48
        number = ref[at : at + 8, lane(2 * half + tile % 2)]
        steps[tile] = number
        frac[tile] = 1.0 / jnp.maximum(number, 1.0)

    def limited(size, half_fraction):
        return size * (0.5 - half_fraction * size)

    def set_up(head, states, first, groups, row):
        def group_rows(i, carry):
            group = first + i
            r = 4 * group + 2
            part = 0.5 * frac[(r + 2) // 8]
            half_fraction = join([part] * PIECES)
            axw[group] = limited(jnp.abs(wx[r - 1]), half_fraction)
            for j in range(4):
                if states is None:
                    for k in range(PIECES):
                        field[r + j, :, lane(k)] = state_row(arrived, half, 4 * i + j, k)
                else:
                    field[r + j] = states[pl.ds(pl.multiple_of(32 * i + 8 * j, 8), 8), :]
                east, north, spread = [
                    jnp.broadcast_to(head[pl.ds(STATE + 16 * q + row + 4 * i + j, 1), :], (8, Y))
                    for q in range(3)
                ]
                wx[r + j] = east
                kk[r + j] = spread
                ax[r + j] = limited(jnp.abs(east), half_fraction)
                south = join(from_left(split(north)))
                forward, backward = jnp.maximum(north, 0.0), jnp.minimum(south, 0.0)
                py[r + j] = forward
                my[r + j] = backward
                pq[r + j] = limited(forward, half_fraction)
                mq[r + j] = limited(-backward, half_fraction)
            return carry

        lax.fori_loop(0, groups, group_rows, 0)

    set_up(low_head, low, 0, REACH // 4, ROWS - REACH)
    set_up(mine, None, REACH // 4, ROWS // 4, 0)
    set_up(high_head, high, (REACH + ROWS) // 4, REACH // 4, 0)

    def flux(w, a, here, there, slope_here, slope_there):
        up = w > 0.0
        return w * jnp.where(up, here, there) + a * jnp.where(up, slope_here, slope_there)

    def outgoing(a, b, value, slope):
        return a * value + b * slope

    def block(substep, source, target, index):
        r = 4 * index + 2
        active = [
            jnp.where(steps[tile] > substep.astype(WIDE), frac[tile], 0.0)
            for tile in ((r + 2) // 8, (r + 6) // 8)
        ]
        c = {i: split(source[r + i]) for i in (-2, -1, 0, 1)}
        dx = {i: minus(c[i + 1], c[i]) for i in (-2, -1, 0)}
        sx = {i: each(minmod, dx[i], dx[i - 1]) for i in (-1, 0)}
        east = None
        for i in range(8):
            c[i + 2] = split(source[r + i + 2])
            dx[i + 1] = minus(c[i + 2], c[i + 1])
            sx[i + 1] = each(minmod, dx[i + 1], dx[i])
            west = east
            if i % 4 == 0:
                a = split(axw[index + i // 4])
                west = each(flux, split(wx[r + i - 1]), a, c[i - 1], c[i], sx[i - 1], sx[i])
            a = split(ax[r + i])
            east = each(flux, split(wx[r + i]), a, c[i], c[i + 1], sx[i], sx[i + 1])
            dy = minus(from_right(c[i]), c[i])
            dy_left = minus(c[i], from_left(c[i]))
            sy = each(minmod, dy, dy_left)
            north = each(outgoing, split(py[r + i]), split(pq[r + i]), c[i], sy)
            south = each(outgoing, split(my[r + i]), split(mq[r + i]), c[i], sy)
            north_left = from_left(north)
            south_right = from_right(south)
            k_row = split(kk[r + i])
            for p in range(PIECES):
                spread = (dx[i][p] - dx[i - 1][p]) + (dy[p] - dy_left[p])
                along = (north_left[p] - north[p]) + (south[p] - south_right[p])
                rate = (west[p] - east[p]) + along + k_row[p] * spread
                target[r + i, :, lane(p)] = c[i][p] + active[i // 4] * rate

    def upwind(w, here, there):
        return w * jnp.where(w > 0.0, here, there)

    def coarse_rows(index, carry):
        r = 4 * index + REACH + 2
        c = {j: split(field[r + j]) for j in range(-1, 5)}
        fx = [each(upwind, split(wx[r + j]), c[j], c[j + 1]) for j in range(-1, 4)]
        for j in range(4):
            right = from_right(c[j])
            left = from_left(c[j])
            north = each(lambda a, b: a * b, split(py[r + j]), c[j])
            south = each(lambda a, b: a * b, split(my[r + j]), c[j])
            north_left = from_left(north)
            south_right = from_right(south)
            k_row = split(kk[r + j])
            for p in range(PIECES):
                spread = c[j - 1][p] + c[j + 1][p] + left[p] + right[p] - 4.0 * c[j][p]
                along = (north_left[p] - north[p]) + (south[p] - south_right[p])
                coarse[4 * index + j, :, lane(p)] = (
                    c[j][p] + (fx[j][p] - fx[j + 1][p]) + along + k_row[p] * spread
                )
        return carry

    lax.fori_loop(0, ROWS // 4, coarse_rows, 0)

    def two_substeps(j, carry):
        for odd, source, target in ((0, field, other), (1, other, field)):
            lax.fori_loop(
                0,
                5 - j - odd,
                lambda i, _: block(2 * j + odd, source, target, j + odd + 2 * i),
                None,
            )
        return carry

    lax.fori_loop(0, SUB // 2, two_substeps, 0)
    out = refs[0] if half == 0 else refs[1]
    if half == 0:
        later = jnp.where(lax.broadcasted_iota(jnp.int32, (8, LANE), 0) > 0, 1.0, 0.0)
    else:
        later = jnp.ones((8, LANE), WIDE)

    def finish(index, carry):
        for j in range(4):
            i = 4 * index + j
            for p in range(PIECES):
                at = (i // 8) * 32 + 8 * p + i % 8
                end = field[REACH + 2 + i, :, lane(p)]
                out[pl.ds(at, 8, stride=64), :] = end - later * coarse[i, :, lane(p)]
        return carry

    lax.fori_loop(0, ROWS // 4, finish, 0)
    if half:
        earlier, _, to_next, to_prev = refs[:4]
        pack(0, earlier, to_next, to_prev)
        pack(1, out, to_next, to_prev)


def pack(half, out, to_next, to_prev):
    base = WIDE_HALO * half
    to_next[base : base + 8, :] = jnp.zeros((8, Y), WIDE)
    used = next_offset(8 * half + 7) + 8 - 8 * half
    total = NARROW_HALO if half else WIDE_HALO
    for ref, filled in ((to_next, used), (to_prev, used - 8)):
        ref[base + filled : base + total, :] = jnp.zeros((total - filled, Y), WIDE)
    for n in range(8 * half, min(8 * half + 8, 15)):
        rows = 15 - n
        for k in range(PIECES):

            def piece(first, last, upper):
                at = (2 * (n - 8 * half) + upper) * 32 + 8 * k
                return out[at + first : at + last, :]

            at = base + next_offset(n)
            if rows > 8:
                to_next[at : at + rows - 8, lane(k)] = piece(16 - rows, 8, 0)
                to_next[at + rows - 8 : at + rows, lane(k)] = piece(0, 8, 1)
            else:
                to_next[at : at + rows, lane(k)] = piece(8 - rows, 8, 1)
            at = base + prev_offset(n)
            if rows > 8:
                to_prev[at : at + 8, lane(k)] = piece(0, 8, 0)
                to_prev[at + 8 : at + rows, lane(k)] = piece(0, rows - 8, 1)
            else:
                to_prev[at : at + rows, lane(k)] = piece(0, rows, 0)


def from_below(tiles):
    row = lax.broadcasted_iota(jnp.int32, (8, LANE), 0)
    turned = [[pltpu.roll(part, 1, 0) for part in tile] for tile in tiles]
    return [
        [jnp.where(row == 0, turned[max(k - 1, 0)][p], turned[k][p]) for p in range(PIECES)]
        for k in range(len(tiles))
    ]


def from_above(tiles):
    row = lax.broadcasted_iota(jnp.int32, (8, LANE), 0)
    turned = [[pltpu.roll(part, 7, 0) for part in tile] for tile in tiles]
    top = len(tiles) - 1
    return [
        [jnp.where(row == 7, turned[min(k + 1, top)][p], turned[k][p]) for p in range(PIECES)]
        for k in range(len(tiles))
    ]


def rows_at(ref, at):
    return split(ref[at : at + 8, :])


def differences(half, n, own, low, high):
    size = 8 if half else 16
    base = WIDE_HALO * half
    tiles = []
    if n < 15:
        at = base + next_offset(n) + 15 - n - size
        tiles += [rows_at(low, at + 8 * k) for k in range(size // 8)]
    at = 16 * (n - 8 * half)
    tiles += [rows_at(own, at), rows_at(own, at + 8)]
    if n < 15:
        at = base + prev_offset(n)
        tiles += [rows_at(high, at + 8 * k) for k in range(size // 8)]
    return tiles


def advance(value, first, added, stencil, inside, keep=None):
    above, below = from_above(value), from_below(value)
    if keep:
        value, above, below = value[keep], above[keep], below[keep]
        first += keep.start
    result = []
    for k in range(len(value)):
        right, left = from_right(value[k]), from_left(value[k])
        parts = []
        for p in range(PIECES):
            a = [stencil[j, pl.ds(8 * (k + first), 8), lane(p)] for j in range(5)]
            moved = (
                (a[0] * value[k][p] + added[k][p])
                + (a[1] * above[k][p] + a[2] * below[k][p])
                + (a[3] * right[p] + a[4] * left[p])
            )
            parts.append(moved * inside if k + first >= 4 else moved)
        result.append(parts)
    return result


def chain_kernel(own, later, mine, low_head, high_head, low, high, out, stencil):
    inside = jnp.where(lax.axis_index("z") < CHIPS - 1, 1.0, 0.0).astype(WIDE)

    def rows_of(q):
        return [
            rows_at(ref, STATE + 16 * q + 8 * upper)
            for ref in (low_head, mine, high_head)
            for upper in range(2)
        ]

    east, north, spread = rows_of(0), rows_of(1), rows_of(2)
    west = from_below(east)
    for k in range(6):
        south = from_left(north[k])
        for p in range(PIECES):
            at = (pl.ds(8 * k, 8), lane(p))
            e, w, n, s, d = east[k][p], west[k][p], north[k][p], south[p], spread[k][p]
            outward = jnp.maximum(e, 0.0) - jnp.minimum(w, 0.0)
            outward = outward + (jnp.maximum(n, 0.0) - jnp.minimum(s, 0.0))
            stencil[0, at[0], at[1]] = 1.0 - outward - 4.0 * d
            stencil[1, at[0], at[1]] = d - jnp.minimum(e, 0.0)
            stencil[2, at[0], at[1]] = d + jnp.maximum(w, 0.0)
            stencil[3, at[0], at[1]] = d - jnp.minimum(n, 0.0)
            stencil[4, at[0], at[1]] = d + jnp.maximum(s, 0.0)

    value = differences(0, 0, own, low, high)
    for n in range(8):
        if n:
            value = advance(value, 0, differences(0, n, own, low, high), stencil, inside)
        for k in range(2):
            out[16 * n + 8 * k : 16 * n + 8 * k + 8, :] = join(value[k + 2])
    value = value[1:5]
    for n in range(8, 16):
        added = differences(1, n, later, low, high)
        keep = slice(1, 3) if n == 15 else None
        value = advance(value, 1, added, stencil, inside, keep)
        for k in range(2):
            at = 16 * n + 8 * k
            out[at : at + 8, :] = join(value[k if keep else k + 1])


def device_at(slab, z, core):
    return (slab * CHIPS + z) * 2 + core


def to_chip(array, step):
    route = [
        (device_at(p, z, c), device_at(p, z + step, c))
        for p in range(SLABS)
        for z in range(CHIPS)
        for c in range(2)
        if 0 <= z + step < CHIPS
    ]
    return lax.ppermute(array, AXES, route)


def on_device(slab_starts, substeps, east_velocity, north_velocity, diffusivity):
    fields = to_tiles(slab_starts.reshape(TR * LEV * X, Y)).reshape(TR * LEV, 32, LANE)
    speeds = [
        to_tiles(a.reshape(LEV * X, Y)).reshape(LEV, 32, LANE)
        for a in (east_velocity, north_velocity, diffusivity)
    ]
    (sent,) = call(
        prepare_kernel,
        [(TR * LEV, CHUNK, LANE)],
        "hhhhh",
        scratch=[
            pltpu.VMEM((LEV, 104, LANE), WIDE),
            pltpu.VMEM((1, 1), jnp.int32),
            pltpu.SemaphoreType.DMA((5,)),
        ],
        flops=300000,
        nbytes=2000000,
        vmem=63 << 20,
    )(substeps, fields, *speeds)
    arrived = lax.all_to_all(sent, ("slab", "core"), 0, 0, tiled=True)
    arrived = arrived.reshape(TR * LEV * CHUNK, LANE)

    head = STATE + 56
    next_a, prev_a = call(functools.partial(arrange_kernel, 0), [(head, Y), (head, Y)], "v")(
        arrived
    )
    low_a, high_a = to_chip(next_a, 1), to_chip(prev_a, -1)
    next_b, prev_b = call(
        functools.partial(arrange_kernel, 1), [(STATE, Y), (STATE, Y)], "vh"
    )(arrived, next_a)
    low_b, high_b = to_chip(next_b, 1), to_chip(prev_b, -1)

    rows = pltpu.VMEM((EXT + 4, 8, Y), WIDE)
    scratch = [
        rows,
        rows,
        pltpu.VMEM((ROWS, 8, Y), WIDE),
        rows,
        rows,
        rows,
        pltpu.VMEM((EXT // 4, 8, Y), WIDE),
        rows,
        rows,
        rows,
        rows,
        pltpu.VMEM((6, 8, LANE), WIDE),
        pltpu.VMEM((6, 8, LANE), WIDE),
    ]
    (own_a,) = call(
        functools.partial(fine_kernel, 0),
        [(512, LANE)],
        "vvvvvv",
        scratch=scratch,
        flops=25000000,
        nbytes=3000000,
    )(arrived, next_a, low_a, high_a, low_a, high_a)
    halo = (WIDE_HALO + NARROW_HALO, Y)
    own_b, next_c, prev_c = call(
        functools.partial(fine_kernel, 1),
        [(512, LANE), halo, halo],
        "vvvvvvv",
        scratch=scratch,
        flops=25000000,
        nbytes=3000000,
    )(arrived, next_a, low_a, high_a, low_b, high_b, own_a)
    low_c, high_c = to_chip(next_c, 1), to_chip(prev_c, -1)
    (chain,) = call(
        chain_kernel,
        [(256, Y)],
        "vvvvvvv",
        scratch=[pltpu.VMEM((5, 48, Y), WIDE)],
        flops=8000000,
    )(from_tiles(own_a), from_tiles(own_b), next_a, low_a, high_a, low_c, high_c)
    result = lax.all_to_all(
        chain.reshape(SLABS * 2, 8, Y), ("slab", "core"), 0, 0, tiled=True
    )
    return result.reshape(1, TR, LEV, X, Y)


def solution(mesh):
    fine_mesh = Mesh(mesh.devices.reshape(SLABS, CHIPS, 2), AXES)
    tile = ("z", "core")
    return jax.shard_map(
        on_device,
        mesh=fine_mesh,
        in_specs=(
            P("slab", None, None, tile, None),
            P("slab", tile),
            P(None, tile, None),
            P(None, tile, None),
            P(None, tile, None),
        ),
        out_specs=P("slab", None, None, tile, None),
        check_vma=False,
    )
```

```python
import functools

import jax
import jax.numpy as jnp
from jax import lax
from jax.experimental import pallas as pl
from jax.experimental.pallas import tpu as pltpu
from jax.sharding import Mesh, PartitionSpec as P

TR, LEV, X, Y = 4, 8, 8, 512
SUB = 6
SLABS = 16
CHIPS = 16
LANE = 128
PIECES = Y // LANE
REACH = 12
ROWS = 2 * X
EXT = ROWS + 2 * REACH
CHUNK = 40
STATE = 8 * REACH
FIRST, REST, HALO = STATE + 3 * REACH + 8, STATE + 3 * (ROWS - REACH), 128
WIDE = jnp.float32
AXES = ("slab", "z", "core")


def split(value):
    return [value[:, LANE * k : LANE * (k + 1)] for k in range(PIECES)]


def join(parts):
    return jnp.concatenate(parts, axis=1)


def lane(k):
    return slice(LANE * k, LANE * (k + 1))


def from_right(parts):
    turned = [pltpu.roll(part, LANE - 1, 1) for part in parts] + [0.0]
    ends = lax.broadcasted_iota(jnp.int32, (8, LANE), 1) == LANE - 1
    return [jnp.where(ends, turned[k + 1], turned[k]) for k in range(PIECES)]


def from_left(parts):
    turned = [pltpu.roll(part, 1, 1) for part in parts] + [0.0]
    ends = lax.broadcasted_iota(jnp.int32, (8, LANE), 1) == 0
    return [jnp.where(ends, turned[k - 1], turned[k]) for k in range(PIECES)]


def minmod(a, b):
    return jnp.maximum(jnp.minimum(a, b), jnp.minimum(jnp.maximum(a, b), 0.0))


def each(function, *lists):
    return [function(*items) for items in zip(*lists)]


def minus(a, b):
    return each(lambda p, q: p - q, a, b)


def call(kernel, shapes, in_specs, scratch=(), flops=1000000, nbytes=1000000, vmem=24 << 20):
    whole = pl.BlockSpec(memory_space=pltpu.VMEM)
    spaces = {
        "v": whole,
        "s": pl.BlockSpec(memory_space=pltpu.SMEM),
        "h": pl.BlockSpec(memory_space=pl.ANY),
    }
    return pl.pallas_call(
        kernel,
        out_shape=[jax.ShapeDtypeStruct(shape, WIDE) for shape in shapes],
        in_specs=[spaces[kind] for kind in in_specs],
        out_specs=[whole] * len(shapes),
        scratch_shapes=list(scratch),
        compiler_params=pltpu.CompilerParams(vmem_limit_bytes=vmem),
        cost_estimate=pl.CostEstimate(flops=flops, bytes_accessed=nbytes, transcendentals=0),
    )


def to_tiles(array):
    rows = array.shape[0] // 8
    return array.reshape(rows, 8, PIECES, LANE).transpose(0, 2, 1, 3)


def from_tiles(array):
    rows = array.shape[0] // (8 * PIECES)
    return array.reshape(rows, PIECES, 8, LANE).transpose(0, 2, 1, 3).reshape(-1, Y)


def prepare_kernel(count_ref, s_ref, e_ref, n_ref, k_ref, out, held, count, sems):
    slab = lax.axis_index("slab")
    copies = [pltpu.make_async_copy(s_ref, out.at[:, pl.ds(0, 32), :], sems.at[0])]
    for q, ref in enumerate((e_ref, n_ref, k_ref)):
        copies.append(
            pltpu.make_async_copy(ref, held.at[:, pl.ds(32 * q, 32), :], sems.at[q + 1])
        )
    copies.append(pltpu.make_async_copy(count_ref, count, sems.at[4]))
    for copy in copies:
        copy.start()
    for copy in copies[1:]:
        copy.wait()
    number = jnp.broadcast_to(count[...].astype(WIDE), (8, LANE))
    row = lax.broadcasted_iota(jnp.int32, (8, LANE), 0)
    held[:, 96:104, :] = jnp.zeros((LEV, 8, LANE), WIDE)
    for level in range(LEV):
        part = held[level, pl.ds(6 * slab, 8), :]
        part = jnp.where(row < 6, part, number)
        for tracer in range(TR):
            out[tracer * LEV + level, 32:40, :] = part
    copies[0].wait()


def state_row(arrived, half, row, k):
    start = (2 * 8 * half + row // 8) * CHUNK + 8 * k + row % 8
    return arrived[pl.ds(start, 8, stride=2 * CHUNK), :]


def arrange_kernel(half, arrived, *refs):
    to_next, to_prev = refs[-2:]
    for i in range(REACH):
        for k in range(PIECES):
            to_next[8 * i : 8 * i + 8, lane(k)] = state_row(arrived, half, i + 4, k)
            to_prev[8 * i : 8 * i + 8, lane(k)] = state_row(arrived, half, i, k)
    if half:
        head = refs[0]
        for q in range(3):
            to_next[STATE + 4 * q : STATE + 4 * q + 4, :] = head[16 * q : 16 * q + 4, :]
            to_prev[STATE + 4 * q : STATE + 4 * q + 4, :] = head[16 * q + 12 : 16 * q + 16, :]
        return
    head = refs[0]
    for n in range(SLABS):
        for core in range(2):
            base = (2 * n + core) * CHUNK + 32
            j = 6 * n
            while j < 6 * n + 6:
                stop = min(6 * n + 6, j // 8 * 8 + 8)
                q, k, x = j // 32, j % 32 // 8, j % 8
                at = 16 * q + 8 * core + x
                head[at : at + stop - j, lane(k)] = arrived[base + j - 6 * n : base + stop - 6 * n, :]
                j = stop
    for core in range(2):
        for group in range(2):
            start = (16 * group + core) * CHUNK + 38
            head[48:56, lane(2 * group + core)] = arrived[pl.ds(start, 8, stride=2 * CHUNK), :]
    for q in range(3):
        at = STATE + REACH * q
        to_next[at : at + REACH, :] = head[16 * q + 4 : 16 * q + 16, :]
        to_prev[at : at + REACH, :] = head[16 * q : 16 * q + REACH, :]
    for ref in (to_next, to_prev):
        ref[FIRST - 8 : FIRST, :] = head[48:56, :]


def next_offset(n):
    return 8 + sum(15 - m for m in range(n))


def prev_offset(n):
    return sum(15 - m for m in range(n + 1, 15))


def fine_kernel(half, arrived, mine, low_head, high_head, low, high, *refs):
    field, other, coarse, wx, kk, ax, axw, wy, ay, steps, frac = refs[-11:]
    for tile in range(6):
        ref, at = ((low_head, FIRST - 8), (mine, 48), (high_head, FIRST - 8))[tile // 2]
        number = ref[at : at + 8, lane(2 * half + tile % 2)]
        steps[tile] = number
        frac[tile] = 1.0 / jnp.maximum(number, 1.0)

    def limited(size, half_fraction):
        return size * (0.5 - half_fraction * size)

    def set_up(head, states, first, groups, row, step):
        def group_rows(i, carry):
            group = first + i
            r = 4 * group + 2
            part = 0.5 * frac[(r + 2) // 8]
            half_fraction = join([part] * PIECES)
            axw[group] = limited(jnp.abs(wx[r - 1]), half_fraction)
            for j in range(4):
                if states is None:
                    for k in range(PIECES):
                        field[r + j, :, lane(k)] = state_row(arrived, half, 4 * i + j, k)
                else:
                    field[r + j] = states[pl.ds(pl.multiple_of(32 * i + 8 * j, 8), 8), :]
                east, north, spread = [
                    jnp.broadcast_to(head[pl.ds(row + step * q + 4 * i + j, 1), :], (8, Y))
                    for q in range(3)
                ]
                wx[r + j] = east
                kk[r + j] = spread
                ax[r + j] = limited(jnp.abs(east), half_fraction)
                wy[r + j] = north
                ay[r + j] = limited(jnp.abs(north), half_fraction)
            return carry

        lax.fori_loop(0, groups, group_rows, 0)

    set_up(low_head, low, 0, REACH // 4, STATE, REACH)
    set_up(mine, None, REACH // 4, ROWS // 4, 0, ROWS)
    set_up(high_head, high, (REACH + ROWS) // 4, REACH // 4, STATE, REACH)

    def flux(w, a, here, there, slope_here, slope_there):
        up = w > 0.0
        return w * jnp.where(up, here, there) + a * jnp.where(up, slope_here, slope_there)

    def block(substep, source, target, index):
        r = 4 * index + 2
        active = [
            jnp.where(steps[tile] > substep.astype(WIDE), frac[tile], 0.0)
            for tile in ((r + 2) // 8, (r + 6) // 8)
        ]
        c = {i: split(source[r + i]) for i in (-2, -1, 0, 1)}
        dx = {i: minus(c[i + 1], c[i]) for i in (-2, -1, 0)}
        sx = {i: each(minmod, dx[i], dx[i - 1]) for i in (-1, 0)}
        east = None
        for i in range(8):
            c[i + 2] = split(source[r + i + 2])
            dx[i + 1] = minus(c[i + 2], c[i + 1])
            sx[i + 1] = each(minmod, dx[i + 1], dx[i])
            west = east
            if i % 4 == 0:
                a = split(axw[index + i // 4])
                west = each(flux, split(wx[r + i - 1]), a, c[i - 1], c[i], sx[i - 1], sx[i])
            a = split(ax[r + i])
            east = each(flux, split(wx[r + i]), a, c[i], c[i + 1], sx[i], sx[i + 1])
            right = from_right(c[i])
            dy = minus(right, c[i])
            dy_left = minus(c[i], from_left(c[i]))
            sy = each(minmod, dy, dy_left)
            north = each(flux, split(wy[r + i]), split(ay[r + i]), c[i], right, sy, from_right(sy))
            south = from_left(north)
            k_row = split(kk[r + i])
            for p in range(PIECES):
                spread = (dx[i][p] - dx[i - 1][p]) + (dy[p] - dy_left[p])
                rate = (west[p] - east[p]) + (south[p] - north[p]) + k_row[p] * spread
                target[r + i, :, lane(p)] = c[i][p] + active[i // 4] * rate

    def upwind(w, here, there):
        return w * jnp.where(w > 0.0, here, there)

    def coarse_rows(index, carry):
        r = 4 * index + REACH + 2
        c = {j: split(field[r + j]) for j in range(-1, 5)}
        fx = [each(upwind, split(wx[r + j]), c[j], c[j + 1]) for j in range(-1, 4)]
        for j in range(4):
            right = from_right(c[j])
            left = from_left(c[j])
            north = each(upwind, split(wy[r + j]), c[j], right)
            south = from_left(north)
            k_row = split(kk[r + j])
            for p in range(PIECES):
                spread = c[j - 1][p] + c[j + 1][p] + left[p] + right[p] - 4.0 * c[j][p]
                along = (fx[j][p] - fx[j + 1][p]) + (south[p] - north[p])
                coarse[4 * index + j, :, lane(p)] = c[j][p] + along + k_row[p] * spread
        return carry

    lax.fori_loop(0, ROWS // 4, coarse_rows, 0)

    def two_substeps(j, carry):
        for odd, source, target in ((0, field, other), (1, other, field)):
            lax.fori_loop(
                0,
                5 - j - odd,
                lambda i, _: block(2 * j + odd, source, target, j + odd + 2 * i),
                None,
            )
        return carry

    lax.fori_loop(0, SUB // 2, two_substeps, 0)
    out = refs[0] if half == 0 else refs[1]
    if half == 0:
        later = jnp.where(lax.broadcasted_iota(jnp.int32, (8, LANE), 0) > 0, 1.0, 0.0)
    else:
        later = jnp.ones((8, LANE), WIDE)

    def finish(index, carry):
        for j in range(4):
            i = 4 * index + j
            for p in range(PIECES):
                at = (i // 8) * 32 + 8 * p + i % 8
                end = field[REACH + 2 + i, :, lane(p)]
                out[pl.ds(at, 8, stride=64), :] = end - later * coarse[i, :, lane(p)]
        return carry

    lax.fori_loop(0, ROWS // 4, finish, 0)
    if half:
        earlier, _, to_next, to_prev = refs[:4]
        pack(0, earlier, to_next, to_prev)
        pack(1, out, to_next, to_prev)


def pack(half, out, to_next, to_prev):
    if half == 0:
        to_next[0:8, :] = jnp.zeros((8, Y), WIDE)
        to_prev[HALO - 8 : HALO, :] = jnp.zeros((8, Y), WIDE)
    for n in range(8 * half, min(8 * half + 8, 15)):
        rows = 15 - n
        for k in range(PIECES):

            def piece(first, last, upper):
                at = (2 * (n - 8 * half) + upper) * 32 + 8 * k
                return out[at + first : at + last, :]

            at = next_offset(n)
            if rows > 8:
                to_next[at : at + rows - 8, lane(k)] = piece(16 - rows, 8, 0)
                to_next[at + rows - 8 : at + rows, lane(k)] = piece(0, 8, 1)
            else:
                to_next[at : at + rows, lane(k)] = piece(8 - rows, 8, 1)
            at = prev_offset(n)
            if rows > 8:
                to_prev[at : at + 8, lane(k)] = piece(0, 8, 0)
                to_prev[at + 8 : at + rows, lane(k)] = piece(0, rows - 8, 1)
            else:
                to_prev[at : at + rows, lane(k)] = piece(0, rows, 0)


def from_below(tiles):
    row = lax.broadcasted_iota(jnp.int32, (8, LANE), 0)
    turned = [[pltpu.roll(part, 1, 0) for part in tile] for tile in tiles]
    return [
        [jnp.where(row == 0, turned[max(k - 1, 0)][p], turned[k][p]) for p in range(PIECES)]
        for k in range(len(tiles))
    ]


def from_above(tiles):
    row = lax.broadcasted_iota(jnp.int32, (8, LANE), 0)
    turned = [[pltpu.roll(part, 7, 0) for part in tile] for tile in tiles]
    top = len(tiles) - 1
    return [
        [jnp.where(row == 7, turned[min(k + 1, top)][p], turned[k][p]) for p in range(PIECES)]
        for k in range(len(tiles))
    ]


def rows_at(ref, at):
    return split(ref[at : at + 8, :])


def differences(half, n, own, low, high):
    size = 8 if half else 16
    tiles = []
    if n < 15:
        at = next_offset(n) + 15 - n - size
        tiles += [rows_at(low, at + 8 * k) for k in range(size // 8)]
    at = 16 * (n - 8 * half)
    tiles += [rows_at(own, at), rows_at(own, at + 8)]
    if n < 15:
        at = prev_offset(n)
        tiles += [rows_at(high, at + 8 * k) for k in range(size // 8)]
    return tiles


def advance(value, first, added, stencil, inside, keep=None):
    above, below = from_above(value), from_below(value)
    if keep:
        value, above, below = value[keep], above[keep], below[keep]
        first += keep.start
    result = []
    for k in range(len(value)):
        right, left = from_right(value[k]), from_left(value[k])
        parts = []
        for p in range(PIECES):
            a = [stencil[j, pl.ds(8 * (k + first), 8), lane(p)] for j in range(5)]
            moved = (
                (a[0] * value[k][p] + added[k][p])
                + (a[1] * above[k][p] + a[2] * below[k][p])
                + (a[3] * right[p] + a[4] * left[p])
            )
            parts.append(moved * inside if k + first >= 4 else moved)
        result.append(parts)
    return result


def chain_kernel(own, later, mine, *refs):
    low_a, high_a, low_b, high_b, low, high, out, stencil, edge = refs
    inside = jnp.where(lax.axis_index("z") < CHIPS - 1, 1.0, 0.0).astype(WIDE)

    for q in range(3):
        edge[0, 16 * q : 16 * q + 4, :] = low_b[STATE + 4 * q : STATE + 4 * q + 4, :]
        edge[1, 16 * q + 12 : 16 * q + 16, :] = high_b[STATE + 4 * q : STATE + 4 * q + 4, :]
        at = STATE + REACH * q
        edge[0, 16 * q + 4 : 16 * q + 16, :] = low_a[at : at + REACH, :]
        edge[1, 16 * q : 16 * q + REACH, :] = high_a[at : at + REACH, :]

    def rows_of(q):
        return [
            rows_at(ref, 16 * q + 8 * upper)
            for ref in (edge.at[0], mine, edge.at[1])
            for upper in range(2)
        ]

    east, north, spread = rows_of(0), rows_of(1), rows_of(2)
    west = from_below(east)
    for k in range(6):
        south = from_left(north[k])
        for p in range(PIECES):
            at = (pl.ds(8 * k, 8), lane(p))
            e, w, n, s, d = east[k][p], west[k][p], north[k][p], south[p], spread[k][p]
            outward = jnp.maximum(e, 0.0) - jnp.minimum(w, 0.0)
            outward = outward + (jnp.maximum(n, 0.0) - jnp.minimum(s, 0.0))
            stencil[0, at[0], at[1]] = 1.0 - outward - 4.0 * d
            stencil[1, at[0], at[1]] = d - jnp.minimum(e, 0.0)
            stencil[2, at[0], at[1]] = d + jnp.maximum(w, 0.0)
            stencil[3, at[0], at[1]] = d - jnp.minimum(n, 0.0)
            stencil[4, at[0], at[1]] = d + jnp.maximum(s, 0.0)

    value = differences(0, 0, own, low, high)
    for n in range(8):
        if n:
            value = advance(value, 0, differences(0, n, own, low, high), stencil, inside)
        for k in range(2):
            out[16 * n + 8 * k : 16 * n + 8 * k + 8, :] = join(value[k + 2])
    value = value[1:5]
    for n in range(8, 16):
        added = differences(1, n, later, low, high)
        keep = slice(1, 3) if n == 15 else None
        value = advance(value, 1, added, stencil, inside, keep)
        for k in range(2):
            at = 16 * n + 8 * k
            out[at : at + 8, :] = join(value[k if keep else k + 1])


def device_at(slab, z, core):
    return (slab * CHIPS + z) * 2 + core


def to_chip(array, step):
    route = [
        (device_at(p, z, c), device_at(p, z + step, c))
        for p in range(SLABS)
        for z in range(CHIPS)
        for c in range(2)
        if 0 <= z + step < CHIPS
    ]
    return lax.ppermute(array, AXES, route)


def on_device(slab_starts, substeps, east_velocity, north_velocity, diffusivity):
    fields = to_tiles(slab_starts.reshape(TR * LEV * X, Y)).reshape(TR * LEV, 32, LANE)
    speeds = [
        to_tiles(a.reshape(LEV * X, Y)).reshape(LEV, 32, LANE)
        for a in (east_velocity, north_velocity, diffusivity)
    ]
    (sent,) = call(
        prepare_kernel,
        [(TR * LEV, CHUNK, LANE)],
        "hhhhh",
        scratch=[
            pltpu.VMEM((LEV, 104, LANE), WIDE),
            pltpu.VMEM((1, 1), jnp.int32),
            pltpu.SemaphoreType.DMA((5,)),
        ],
        flops=300000,
        nbytes=2000000,
        vmem=63 << 20,
    )(substeps, fields, *speeds)
    arrived = lax.all_to_all(sent, ("slab", "core"), 0, 0, tiled=True)
    arrived = arrived.reshape(TR * LEV * CHUNK, LANE)

    mine, next_a, prev_a = call(
        functools.partial(arrange_kernel, 0), [(56, Y), (FIRST, Y), (FIRST, Y)], "v"
    )(arrived)
    low_a, high_a = to_chip(next_a, 1), to_chip(prev_a, -1)
    next_b, prev_b = call(
        functools.partial(arrange_kernel, 1), [(REST, Y), (REST, Y)], "vv"
    )(arrived, mine)
    low_b, high_b = to_chip(next_b, 1), to_chip(prev_b, -1)

    rows = pltpu.VMEM((EXT + 4, 8, Y), WIDE)
    scratch = [
        rows,
        rows,
        pltpu.VMEM((ROWS, 8, Y), WIDE),
        rows,
        rows,
        rows,
        pltpu.VMEM((EXT // 4, 8, Y), WIDE),
        rows,
        rows,
        pltpu.VMEM((6, 8, LANE), WIDE),
        pltpu.VMEM((6, 8, LANE), WIDE),
    ]
    (own_a,) = call(
        functools.partial(fine_kernel, 0),
        [(512, LANE)],
        "vvvvvv",
        scratch=scratch,
        flops=25000000,
        nbytes=3000000,
    )(arrived, mine, low_a, high_a, low_a, high_a)
    halo = (HALO, Y)
    own_b, next_c, prev_c = call(
        functools.partial(fine_kernel, 1),
        [(512, LANE), halo, halo],
        "vvvvvvv",
        scratch=scratch,
        flops=25000000,
        nbytes=3000000,
    )(arrived, mine, low_a, high_a, low_b, high_b, own_a)
    low_c, high_c = to_chip(next_c, 1), to_chip(prev_c, -1)
    (chain,) = call(
        chain_kernel,
        [(256, Y)],
        "vvvvvvvvv",
        scratch=[pltpu.VMEM((5, 48, Y), WIDE), pltpu.VMEM((2, 48, Y), WIDE)],
        flops=8000000,
    )(from_tiles(own_a), from_tiles(own_b), mine, low_a, high_a, low_b, high_b, low_c, high_c)
    result = lax.all_to_all(
        chain.reshape(SLABS * 2, 8, Y), ("slab", "core"), 0, 0, tiled=True
    )
    return result.reshape(1, TR, LEV, X, Y)


def solution(mesh):
    fine_mesh = Mesh(mesh.devices.reshape(SLABS, CHIPS, 2), AXES)
    tile = ("z", "core")
    return jax.shard_map(
        on_device,
        mesh=fine_mesh,
        in_specs=(
            P("slab", None, None, tile, None),
            P("slab", tile),
            P(None, tile, None),
            P(None, tile, None),
            P(None, tile, None),
        ),
        out_specs=P("slab", None, None, tile, None),
        check_vma=False,
    )
```

```python
import functools

import jax
import jax.numpy as jnp
from jax import lax
from jax.experimental import pallas as pl
from jax.experimental.pallas import tpu as pltpu
from jax.sharding import Mesh, PartitionSpec as P

TR, LEV, X, Y = 4, 8, 8, 512
SUB = 6
SLABS = 16
CHIPS = 16
LANE = 128
PIECES = Y // LANE
REACH = 12
ROWS = 2 * X
EXT = ROWS + 2 * REACH
CHUNK = 40
STATE = 8 * REACH
FIRST, REST, HALO = STATE + 3 * REACH + 8, STATE + 3 * (ROWS - REACH), 120
WIDE = jnp.float32
AXES = ("slab", "z", "core")


def split(value):
    return [value[:, LANE * k : LANE * (k + 1)] for k in range(PIECES)]


def join(parts):
    return jnp.concatenate(parts, axis=1)


def lane(k):
    return slice(LANE * k, LANE * (k + 1))


def from_right(parts):
    turned = [pltpu.roll(part, LANE - 1, 1) for part in parts] + [0.0]
    ends = lax.broadcasted_iota(jnp.int32, (8, LANE), 1) == LANE - 1
    return [jnp.where(ends, turned[k + 1], turned[k]) for k in range(PIECES)]


def from_left(parts):
    turned = [pltpu.roll(part, 1, 1) for part in parts] + [0.0]
    ends = lax.broadcasted_iota(jnp.int32, (8, LANE), 1) == 0
    return [jnp.where(ends, turned[k - 1], turned[k]) for k in range(PIECES)]


def minmod(a, b):
    return jnp.maximum(jnp.minimum(a, b), jnp.minimum(jnp.maximum(a, b), 0.0))


def each(function, *lists):
    return [function(*items) for items in zip(*lists)]


def minus(a, b):
    return each(lambda p, q: p - q, a, b)


def call(kernel, shapes, in_specs, scratch=(), flops=1000000, nbytes=1000000, vmem=24 << 20):
    whole = pl.BlockSpec(memory_space=pltpu.VMEM)
    spaces = {
        "v": whole,
        "s": pl.BlockSpec(memory_space=pltpu.SMEM),
        "h": pl.BlockSpec(memory_space=pl.ANY),
    }
    return pl.pallas_call(
        kernel,
        out_shape=[jax.ShapeDtypeStruct(shape, WIDE) for shape in shapes],
        in_specs=[spaces[kind] for kind in in_specs],
        out_specs=[whole] * len(shapes),
        scratch_shapes=list(scratch),
        compiler_params=pltpu.CompilerParams(vmem_limit_bytes=vmem),
        cost_estimate=pl.CostEstimate(flops=flops, bytes_accessed=nbytes, transcendentals=0),
    )


def to_tiles(array):
    rows = array.shape[0] // 8
    return array.reshape(rows, 8, PIECES, LANE).transpose(0, 2, 1, 3)


def from_tiles(array):
    rows = array.shape[0] // (8 * PIECES)
    return array.reshape(rows, PIECES, 8, LANE).transpose(0, 2, 1, 3).reshape(-1, Y)


def prepare_kernel(count_ref, s_ref, e_ref, n_ref, k_ref, out, held, count, sems):
    slab = lax.axis_index("slab")
    copies = [pltpu.make_async_copy(s_ref, out.at[:, pl.ds(0, 32), :], sems.at[0])]
    for q, ref in enumerate((e_ref, n_ref, k_ref)):
        copies.append(
            pltpu.make_async_copy(ref, held.at[:, pl.ds(32 * q, 32), :], sems.at[q + 1])
        )
    copies.append(pltpu.make_async_copy(count_ref, count, sems.at[4]))
    for copy in copies:
        copy.start()
    for copy in copies[1:]:
        copy.wait()
    number = jnp.broadcast_to(count[...].astype(WIDE), (8, LANE))
    row = lax.broadcasted_iota(jnp.int32, (8, LANE), 0)
    held[:, 96:104, :] = jnp.zeros((LEV, 8, LANE), WIDE)
    for level in range(LEV):
        part = held[level, pl.ds(6 * slab, 8), :]
        part = jnp.where(row < 6, part, number)
        for tracer in range(TR):
            out[tracer * LEV + level, 32:40, :] = part
    copies[0].wait()


def state_row(arrived, half, row, k):
    start = (2 * 8 * half + row // 8) * CHUNK + 8 * k + row % 8
    return arrived[pl.ds(start, 8, stride=2 * CHUNK), :]


def arrange_kernel(half, arrived, *refs):
    to_next, to_prev = refs[-2:]
    for i in range(REACH):
        for k in range(PIECES):
            to_next[8 * i : 8 * i + 8, lane(k)] = state_row(arrived, half, i + 4, k)
            to_prev[8 * i : 8 * i + 8, lane(k)] = state_row(arrived, half, i, k)
    if half:
        head = refs[0]
        for q in range(3):
            to_next[STATE + 4 * q : STATE + 4 * q + 4, :] = head[16 * q : 16 * q + 4, :]
            to_prev[STATE + 4 * q : STATE + 4 * q + 4, :] = head[16 * q + 12 : 16 * q + 16, :]
        return
    head = refs[0]
    for n in range(SLABS):
        for core in range(2):
            base = (2 * n + core) * CHUNK + 32
            j = 6 * n
            while j < 6 * n + 6:
                stop = min(6 * n + 6, j // 8 * 8 + 8)
                q, k, x = j // 32, j % 32 // 8, j % 8
                at = 16 * q + 8 * core + x
                head[at : at + stop - j, lane(k)] = arrived[base + j - 6 * n : base + stop - 6 * n, :]
                j = stop
    for core in range(2):
        for group in range(2):
            start = (16 * group + core) * CHUNK + 38
            head[48:56, lane(2 * group + core)] = arrived[pl.ds(start, 8, stride=2 * CHUNK), :]
    for q in range(3):
        at = STATE + REACH * q
        to_next[at : at + REACH, :] = head[16 * q + 4 : 16 * q + 16, :]
        to_prev[at : at + REACH, :] = head[16 * q : 16 * q + REACH, :]
    for ref in (to_next, to_prev):
        ref[FIRST - 8 : FIRST, :] = head[48:56, :]


def next_offset(n):
    return sum(15 - m for m in range(n))


def prev_offset(n):
    return sum(15 - m for m in range(n + 1, 15))


def fine_kernel(half, arrived, mine, low_head, high_head, low, high, *refs):
    field, other, coarse, wx, kk, ax, axw, wy, ay, steps, frac = refs[-11:]
    for tile in range(6):
        ref, at = ((low_head, FIRST - 8), (mine, 48), (high_head, FIRST - 8))[tile // 2]
        number = ref[at : at + 8, lane(2 * half + tile % 2)]
        steps[tile] = number
        frac[tile] = 1.0 / jnp.maximum(number, 1.0)

    def limited(size, half_fraction):
        return size * (0.5 - half_fraction * size)

    def set_up(head, states, first, groups, row, step):
        def group_rows(i, carry):
            group = first + i
            r = 4 * group + 2
            part = 0.5 * frac[(r + 2) // 8]
            half_fraction = join([part] * PIECES)
            axw[group] = limited(jnp.abs(wx[r - 1]), half_fraction)
            for j in range(4):
                if states is None:
                    for k in range(PIECES):
                        field[r + j, :, lane(k)] = state_row(arrived, half, 4 * i + j, k)
                else:
                    field[r + j] = states[pl.ds(pl.multiple_of(32 * i + 8 * j, 8), 8), :]
                east, north, spread = [
                    jnp.broadcast_to(head[pl.ds(row + step * q + 4 * i + j, 1), :], (8, Y))
                    for q in range(3)
                ]
                wx[r + j] = east
                kk[r + j] = spread
                ax[r + j] = limited(jnp.abs(east), half_fraction)
                wy[r + j] = north
                ay[r + j] = limited(jnp.abs(north), half_fraction)
            return carry

        lax.fori_loop(0, groups, group_rows, 0)

    set_up(low_head, low, 0, REACH // 4, STATE, REACH)
    set_up(mine, None, REACH // 4, ROWS // 4, 0, ROWS)
    set_up(high_head, high, (REACH + ROWS) // 4, REACH // 4, STATE, REACH)

    def flux(w, a, here, there, slope_here, slope_there):
        up = w > 0.0
        return w * jnp.where(up, here, there) + a * jnp.where(up, slope_here, slope_there)

    def block(substep, source, target, index):
        r = 4 * index + 2
        active = [
            jnp.where(steps[tile] > substep.astype(WIDE), frac[tile], 0.0)
            for tile in ((r + 2) // 8, (r + 6) // 8)
        ]
        c = {i: split(source[r + i]) for i in (-2, -1, 0, 1)}
        dx = {i: minus(c[i + 1], c[i]) for i in (-2, -1, 0)}
        sx = {i: each(minmod, dx[i], dx[i - 1]) for i in (-1, 0)}
        east = None
        for i in range(8):
            c[i + 2] = split(source[r + i + 2])
            dx[i + 1] = minus(c[i + 2], c[i + 1])
            sx[i + 1] = each(minmod, dx[i + 1], dx[i])
            west = east
            if i % 4 == 0:
                a = split(axw[index + i // 4])
                west = each(flux, split(wx[r + i - 1]), a, c[i - 1], c[i], sx[i - 1], sx[i])
            a = split(ax[r + i])
            east = each(flux, split(wx[r + i]), a, c[i], c[i + 1], sx[i], sx[i + 1])
            right = from_right(c[i])
            dy = minus(right, c[i])
            dy_left = minus(c[i], from_left(c[i]))
            sy = each(minmod, dy, dy_left)
            north = each(flux, split(wy[r + i]), split(ay[r + i]), c[i], right, sy, from_right(sy))
            south = from_left(north)
            k_row = split(kk[r + i])
            for p in range(PIECES):
                spread = (dx[i][p] - dx[i - 1][p]) + (dy[p] - dy_left[p])
                rate = (west[p] - east[p]) + (south[p] - north[p]) + k_row[p] * spread
                target[r + i, :, lane(p)] = c[i][p] + active[i // 4] * rate

    def upwind(w, here, there):
        return w * jnp.where(w > 0.0, here, there)

    def coarse_rows(index, carry):
        r = 4 * index + REACH + 2
        c = {j: split(field[r + j]) for j in range(-1, 5)}
        fx = [each(upwind, split(wx[r + j]), c[j], c[j + 1]) for j in range(-1, 4)]
        for j in range(4):
            right = from_right(c[j])
            left = from_left(c[j])
            north = each(upwind, split(wy[r + j]), c[j], right)
            south = from_left(north)
            k_row = split(kk[r + j])
            for p in range(PIECES):
                spread = c[j - 1][p] + c[j + 1][p] + left[p] + right[p] - 4.0 * c[j][p]
                along = (fx[j][p] - fx[j + 1][p]) + (south[p] - north[p])
                coarse[4 * index + j, :, lane(p)] = c[j][p] + along + k_row[p] * spread
        return carry

    lax.fori_loop(0, ROWS // 4, coarse_rows, 0)

    def two_substeps(j, carry):
        for odd, source, target in ((0, field, other), (1, other, field)):
            lax.fori_loop(
                0,
                5 - j - odd,
                lambda i, _: block(2 * j + odd, source, target, j + odd + 2 * i),
                None,
            )
        return carry

    lax.fori_loop(0, SUB // 2, two_substeps, 0)
    out = refs[0] if half == 0 else refs[1]
    if half == 0:
        later = jnp.where(lax.broadcasted_iota(jnp.int32, (8, LANE), 0) > 0, 1.0, 0.0)
    else:
        later = jnp.ones((8, LANE), WIDE)

    def finish(index, carry):
        for j in range(4):
            i = 4 * index + j
            for p in range(PIECES):
                at = (i // 8) * 32 + 8 * p + i % 8
                end = field[REACH + 2 + i, :, lane(p)]
                out[pl.ds(at, 8, stride=64), :] = end - later * coarse[i, :, lane(p)]
        return carry

    lax.fori_loop(0, ROWS // 4, finish, 0)
    if half:
        earlier, _, to_next, to_prev = refs[:4]
        pack(0, earlier, to_next, to_prev)
        pack(1, out, to_next, to_prev)


def pack(half, out, to_next, to_prev):
    for n in range(8 * half, min(8 * half + 8, 15)):
        rows = 15 - n
        for k in range(PIECES):

            def piece(first, last, upper):
                at = (2 * (n - 8 * half) + upper) * 32 + 8 * k
                return out[at + first : at + last, :]

            at = next_offset(n)
            if rows > 8:
                to_next[at : at + rows - 8, lane(k)] = piece(16 - rows, 8, 0)
                to_next[at + rows - 8 : at + rows, lane(k)] = piece(0, 8, 1)
            else:
                to_next[at : at + rows, lane(k)] = piece(8 - rows, 8, 1)
            at = prev_offset(n)
            if rows > 8:
                to_prev[at : at + 8, lane(k)] = piece(0, 8, 0)
                to_prev[at + 8 : at + rows, lane(k)] = piece(0, rows - 8, 1)
            else:
                to_prev[at : at + rows, lane(k)] = piece(0, rows, 0)


def from_below(tiles):
    row = lax.broadcasted_iota(jnp.int32, (8, LANE), 0)
    turned = [[pltpu.roll(part, 1, 0) for part in tile] for tile in tiles]
    return [
        [jnp.where(row == 0, turned[max(k - 1, 0)][p], turned[k][p]) for p in range(PIECES)]
        for k in range(len(tiles))
    ]


def from_above(tiles):
    row = lax.broadcasted_iota(jnp.int32, (8, LANE), 0)
    turned = [[pltpu.roll(part, 7, 0) for part in tile] for tile in tiles]
    top = len(tiles) - 1
    return [
        [jnp.where(row == 7, turned[min(k + 1, top)][p], turned[k][p]) for p in range(PIECES)]
        for k in range(len(tiles))
    ]


def rows_at(ref, at):
    return split(ref[at : at + 8, :])


def rows_inside(ref, at):
    begin = min(max(at, 0), HALO - 8)
    tile = rows_at(ref, begin)
    return [pltpu.roll(part, (begin - at) % 8, 0) for part in tile] if begin != at else tile


def differences(half, n, own, low, high):
    size = 8 if half else 16
    tiles = []
    if n < 15:
        at = next_offset(n) + 15 - n - size
        tiles += [rows_inside(low, at + 8 * k) for k in range(size // 8)]
    at = 16 * (n - 8 * half)
    tiles += [rows_at(own, at), rows_at(own, at + 8)]
    if n < 15:
        at = prev_offset(n)
        tiles += [rows_inside(high, at + 8 * k) for k in range(size // 8)]
    return tiles


def advance(value, first, added, stencil, inside, keep=None):
    above, below = from_above(value), from_below(value)
    if keep:
        value, above, below = value[keep], above[keep], below[keep]
        first += keep.start
    result = []
    for k in range(len(value)):
        right, left = from_right(value[k]), from_left(value[k])
        parts = []
        for p in range(PIECES):
            a = [stencil[j, pl.ds(8 * (k + first), 8), lane(p)] for j in range(5)]
            moved = (
                (a[0] * value[k][p] + added[k][p])
                + (a[1] * above[k][p] + a[2] * below[k][p])
                + (a[3] * right[p] + a[4] * left[p])
            )
            parts.append(moved * inside if k + first >= 4 else moved)
        result.append(parts)
    return result


def chain_kernel(own, later, mine, *refs):
    low_a, high_a, low_b, high_b, low, high, out, stencil, edge = refs
    inside = jnp.where(lax.axis_index("z") < CHIPS - 1, 1.0, 0.0).astype(WIDE)

    for q in range(3):
        edge[0, 16 * q : 16 * q + 4, :] = low_b[STATE + 4 * q : STATE + 4 * q + 4, :]
        edge[1, 16 * q + 12 : 16 * q + 16, :] = high_b[STATE + 4 * q : STATE + 4 * q + 4, :]
        at = STATE + REACH * q
        edge[0, 16 * q + 4 : 16 * q + 16, :] = low_a[at : at + REACH, :]
        edge[1, 16 * q : 16 * q + REACH, :] = high_a[at : at + REACH, :]

    def rows_of(q):
        return [
            rows_at(ref, 16 * q + 8 * upper)
            for ref in (edge.at[0], mine, edge.at[1])
            for upper in range(2)
        ]

    east, north, spread = rows_of(0), rows_of(1), rows_of(2)
    west = from_below(east)
    for k in range(6):
        south = from_left(north[k])
        for p in range(PIECES):
            at = (pl.ds(8 * k, 8), lane(p))
            e, w, n, s, d = east[k][p], west[k][p], north[k][p], south[p], spread[k][p]
            outward = jnp.maximum(e, 0.0) - jnp.minimum(w, 0.0)
            outward = outward + (jnp.maximum(n, 0.0) - jnp.minimum(s, 0.0))
            stencil[0, at[0], at[1]] = 1.0 - outward - 4.0 * d
            stencil[1, at[0], at[1]] = d - jnp.minimum(e, 0.0)
            stencil[2, at[0], at[1]] = d + jnp.maximum(w, 0.0)
            stencil[3, at[0], at[1]] = d - jnp.minimum(n, 0.0)
            stencil[4, at[0], at[1]] = d + jnp.maximum(s, 0.0)

    value = differences(0, 0, own, low, high)
    for n in range(8):
        if n:
            value = advance(value, 0, differences(0, n, own, low, high), stencil, inside)
        for k in range(2):
            out[16 * n + 8 * k : 16 * n + 8 * k + 8, :] = join(value[k + 2])
    value = value[1:5]
    for n in range(8, 16):
        added = differences(1, n, later, low, high)
        keep = slice(1, 3) if n == 15 else None
        value = advance(value, 1, added, stencil, inside, keep)
        for k in range(2):
            at = 16 * n + 8 * k
            out[at : at + 8, :] = join(value[k if keep else k + 1])


def device_at(slab, z, core):
    return (slab * CHIPS + z) * 2 + core


def to_chip(array, step):
    route = [
        (device_at(p, z, c), device_at(p, z + step, c))
        for p in range(SLABS)
        for z in range(CHIPS)
        for c in range(2)
        if 0 <= z + step < CHIPS
    ]
    return lax.ppermute(array, AXES, route)


def on_device(slab_starts, substeps, east_velocity, north_velocity, diffusivity):
    fields = to_tiles(slab_starts.reshape(TR * LEV * X, Y)).reshape(TR * LEV, 32, LANE)
    speeds = [
        to_tiles(a.reshape(LEV * X, Y)).reshape(LEV, 32, LANE)
        for a in (east_velocity, north_velocity, diffusivity)
    ]
    (sent,) = call(
        prepare_kernel,
        [(TR * LEV, CHUNK, LANE)],
        "hhhhh",
        scratch=[
            pltpu.VMEM((LEV, 104, LANE), WIDE),
            pltpu.VMEM((1, 1), jnp.int32),
            pltpu.SemaphoreType.DMA((5,)),
        ],
        flops=300000,
        nbytes=2000000,
        vmem=63 << 20,
    )(substeps, fields, *speeds)
    arrived = lax.all_to_all(sent, ("slab", "core"), 0, 0, tiled=True)
    arrived = arrived.reshape(TR * LEV * CHUNK, LANE)

    mine, next_a, prev_a = call(
        functools.partial(arrange_kernel, 0), [(56, Y), (FIRST, Y), (FIRST, Y)], "v"
    )(arrived)
    low_a, high_a = to_chip(next_a, 1), to_chip(prev_a, -1)
    next_b, prev_b = call(
        functools.partial(arrange_kernel, 1), [(REST, Y), (REST, Y)], "vv"
    )(arrived, mine)
    low_b, high_b = to_chip(next_b, 1), to_chip(prev_b, -1)

    rows = pltpu.VMEM((EXT + 4, 8, Y), WIDE)
    scratch = [
        rows,
        rows,
        pltpu.VMEM((ROWS, 8, Y), WIDE),
        rows,
        rows,
        rows,
        pltpu.VMEM((EXT // 4, 8, Y), WIDE),
        rows,
        rows,
        pltpu.VMEM((6, 8, LANE), WIDE),
        pltpu.VMEM((6, 8, LANE), WIDE),
    ]
    (own_a,) = call(
        functools.partial(fine_kernel, 0),
        [(512, LANE)],
        "vvvvvv",
        scratch=scratch,
        flops=25000000,
        nbytes=3000000,
    )(arrived, mine, low_a, high_a, low_a, high_a)
    halo = (HALO, Y)
    own_b, next_c, prev_c = call(
        functools.partial(fine_kernel, 1),
        [(512, LANE), halo, halo],
        "vvvvvvv",
        scratch=scratch,
        flops=25000000,
        nbytes=3000000,
    )(arrived, mine, low_a, high_a, low_b, high_b, own_a)
    low_c, high_c = to_chip(next_c, 1), to_chip(prev_c, -1)
    (chain,) = call(
        chain_kernel,
        [(256, Y)],
        "vvvvvvvvv",
        scratch=[pltpu.VMEM((5, 48, Y), WIDE), pltpu.VMEM((2, 48, Y), WIDE)],
        flops=8000000,
    )(from_tiles(own_a), from_tiles(own_b), mine, low_a, high_a, low_b, high_b, low_c, high_c)
    result = lax.all_to_all(
        chain.reshape(SLABS * 2, 8, Y), ("slab", "core"), 0, 0, tiled=True
    )
    return result.reshape(1, TR, LEV, X, Y)


def solution(mesh):
    fine_mesh = Mesh(mesh.devices.reshape(SLABS, CHIPS, 2), AXES)
    tile = ("z", "core")
    return jax.shard_map(
        on_device,
        mesh=fine_mesh,
        in_specs=(
            P("slab", None, None, tile, None),
            P("slab", tile),
            P(None, tile, None),
            P(None, tile, None),
            P(None, tile, None),
        ),
        out_specs=P("slab", None, None, tile, None),
        check_vma=False,
    )
```
